256 devices in a mesh: grp: 4 (over y_hi, core), idx: 64 (over x, z, y_lo).
Axes of the slice: x: 4, y: 4 (y_hi: 2, y_lo: 2; y = y_hi * 2 + y_lo), z: 8, core: 2. Of those that a mesh axis runs over, the one named last changes fastest.
Arguments:
- queries: bfloat16 [4096, 1024], P(('grp', 'idx')), may hold values from -14 to 14
- exemplars: bfloat16 [262144, 1024], P('idx'), may hold values from -4 to 4
- labels: int32 [262144, 64], P('idx'), may hold values 0 or 1
Outputs:
- risk: float32 [4096, 64], P(('grp', 'idx'))
- density: float32 [4096], P(('grp', 'idx'))
The draws below stay inside these ranges and needn't reach their ends.
All inputs are finite; a program needn't handle non-finite values. No bound on the sum of `labels` on one device may be relied on, other than what follows from the above.
Results may differ from the reference program's by a relative error of at most 0.004.
Values may be sent and summed in bfloat16 or wider, within the bound.
A program may use at most 128 MiB of HBM per device.

```python
import math
import jax
import jax.numpy as jnp
from jax import lax

D = 1024
C = 64
NQ = 4096
NE = 262144


def exemplar_block(base_key, row_ids):

    def one_row(row_number):
        row_key = jax.random.fold_in(base_key, row_number)
        vector = jnp.clip(jax.random.normal(row_key, (D,), jnp.float32), -4.0, 4.0)
        return vector
    return jax.vmap(one_row)(row_ids)


def draw_exemplars(key, part):
    base_key = jax.random.fold_in(key, 11)
    return exemplar_block(base_key, jnp.arange(NE, dtype=jnp.int32)).astype(jnp.bfloat16)


def draw_queries(key, part):
    base_key = jax.random.fold_in(key, 11)
    drawn = jnp.clip(jax.random.normal(jax.random.fold_in(key, 23), (NQ, D), jnp.float32), -4.0, 4.0)
    chosen_rows = jax.random.randint(jax.random.fold_in(key, 29), (NQ, 2), 0, NE)
    strength = jax.random.uniform(jax.random.fold_in(key, 31), (NQ, 1), jnp.float32, 1.1, 2.4)
    pair_sum = exemplar_block(base_key, chosen_rows[:, 0]) + exemplar_block(base_key, chosen_rows[:, 1])
    aligned = (jnp.arange(NQ) % 61 == 7)[:, None]
    drawn = jnp.where(aligned, jnp.clip(strength * pair_sum, -13.9, 13.9), drawn)
    return drawn.astype(jnp.bfloat16)


def with_ends(result, stream_key, low, largest):
    longest = result.shape.index(max(result.shape))
    spots = []
    for shift in (0, 1):
        where = [jax.random.randint(jax.random.fold_in(stream_key, axis), (), 0, length) for axis, length in enumerate(result.shape)]
        where[longest] = (where[longest] + shift) % result.shape[longest]
        spots.append(tuple(where))
    return result.at[spots[0]].set(low).at[spots[1]].set(largest)


def setup_inputs(seed: int = 0) -> dict:
    key_of = jax.random.split(jax.random.key(seed), 4)
    queries = draw_queries(jax.random.fold_in(key_of[3], 71), 0)
    exemplars = draw_exemplars(jax.random.fold_in(key_of[3], 71), 0)
    labels = with_ends((jax.random.randint(key_of[2], (NE, C), 0, 8) < 1).astype(jnp.int32), jax.random.fold_in(key_of[2], 1), 0, 1)
    return {"queries": queries, "exemplars": exemplars, "labels": labels}


def reference(queries, exemplars, labels):
    total_q = queries.shape[0]
    total_e = exemplars.shape[0]
    score_gain = 3.0 / math.sqrt(D)
    block_rows = math.gcd(total_q, 512)
    blocked = queries.reshape(total_q // block_rows, block_rows, D)
    label_values = labels.astype(jnp.bfloat16)

    def block_scores(block):
        return jnp.dot(block, exemplars.T, preferred_element_type=jnp.float32) * score_gain

    def first_pass(carry, block):
        col_max, col_sum = carry
        scores = block_scores(block)
        row_max = lax.optimization_barrier(jnp.max(scores, axis=1))
        row_dens = row_max + jnp.log(lax.optimization_barrier(jnp.sum(jnp.exp(scores - row_max[:, None]), axis=1))) - math.log(total_e)
        block_max = lax.optimization_barrier(jnp.max(scores, axis=0))
        new_max = jnp.maximum(col_max, block_max)
        new_sum = col_sum * jnp.exp(col_max - new_max) + lax.optimization_barrier(jnp.sum(jnp.exp(scores - block_max[None, :]), axis=0)) * jnp.exp(block_max - new_max)
        return ((new_max, new_sum), row_dens)
    start = (jnp.full((total_e,), -1e+30, jnp.float32), jnp.zeros((total_e,), jnp.float32))
    (col_max, col_sum), dens_blocks = lax.scan(first_pass, start, blocked)
    hub = col_max + jnp.log(col_sum) - math.log(total_q)

    def second_pass(block):
        scores = block_scores(block)
        corrected = 2.0 * scores - hub[None, :]
        row_top = lax.optimization_barrier(jnp.max(corrected, axis=1))
        weights = jnp.exp(corrected - row_top[:, None])
        weight_sum = lax.optimization_barrier(jnp.sum(weights, axis=1))
        numerator = jnp.dot(weights.astype(jnp.bfloat16), label_values, preferred_element_type=jnp.float32)
        return numerator / weight_sum[:, None]
    risk = lax.map(second_pass, blocked).reshape(total_q, C)
    return (risk, dens_blocks.reshape(total_q))
```

```python
import functools
import math

import jax
import jax.numpy as jnp
from jax import lax
from jax.experimental import pallas as pl
from jax.experimental.pallas import tpu as pltpu
from jax.sharding import PartitionSpec as P

X, Z, Y, GROUPS = 4, 8, 2, 4
SHARD = 16
X_ORDER = (0, 1, -1, 2)
Z_ORDER = (0, 1, -1, 2, -2, 3, -3, 4)
FIRST_BASE = {0: 0, 1: 64, -1: 128, 2: 576, -2: 640, 3: 832, -3: 896, 4: 960}
SECOND_BASE = {0: 192, 1: 320, -1: 448, 2: 704}
PIECES = ((0, 1), (1, 2), (3, 2), (5, 2), (7, 1))
BLOCK = 256
WIDE = 1024
CATEGORIES = 64
MASS, TOP, DENS = 64, 65, 66
PACKED = 72
LOG2E = 1.4426950408889634
LOWEST = -1e30
MESH = pl.DeviceIdType.MESH


def row_of(side, dx, dz):
    if side == 0:
        return FIRST_BASE[dz] + SHARD * X_ORDER.index(dx)
    return SECOND_BASE[dx] + SHARD * Z_ORDER.index(dz)


def gather_moves():
    moves = {}
    moves["x+"] = (row_of(0, 0, 0), 1, row_of(0, -1, 0), "xp")
    moves["x-"] = (row_of(0, 0, 0), 1, row_of(0, 1, 0), "xm")
    moves["x2"] = (row_of(0, -1, 0), 1, row_of(0, 2, 0), "xp")
    for k in (1, 2, 3, 4):
        far = 4 if k == 4 else -k
        for half in (0, 1):
            off = 32 * half
            if k < 4 or half == 0:
                moves["z+", k, half] = (FIRST_BASE[1 - k] + off, 2, FIRST_BASE[far] + off, "zp")
            if k < 4 or half == 1:
                moves["z-", k, half] = (FIRST_BASE[k - 1] + off, 2, FIRST_BASE[k] + off, "zm")
        moves["w+", k] = (row_of(1, 0, 1 - k), 1, row_of(1, 0, far), "zp")
        if k < 4:
            moves["w-", k] = (row_of(1, 0, k - 1), 1, row_of(1, 0, k), "zm")
    for g, (start, count) in enumerate(PIECES):
        off = SHARD * start
        moves["v+", g] = (SECOND_BASE[0] + off, count, SECOND_BASE[-1] + off, "xp")
        moves["v-", g] = (SECOND_BASE[0] + off, count, SECOND_BASE[1] + off, "xm")
        if g in (0, 1, 4):
            moves["u+", g] = (SECOND_BASE[-1] + off, count, SECOND_BASE[2] + off, "xp")
        else:
            moves["u-", g] = (SECOND_BASE[1] + off, count, SECOND_BASE[2] + off, "xm")
    return moves


MOVES = gather_moves()
MOVE_IDS = {name: 1 + i for i, name in enumerate(MOVES)}
N_MOVES = 1 + len(MOVES)


def dot_t(a, b):
    return lax.dot_general(a, b, (((1,), (1,)), ((), ())), preferred_element_type=jnp.float32)


def kernel(
    groups, total_q, total_e,
    q_ref, ex_hbm, labels_hbm, risk_ref, density_ref,
    rows, ex, labels_raw, labels, s0, s1, s2, s3,
    top_part0, top_part1, row_top, row_sum, peak0, peak1, col_max, col_sum,
    hubs, hub_row, numer, packed, arrived, spread, last,
    load_sem, send, recv, hub_send, hub_recv, a_send, a_recv, b_send, b_recv,
):
    scores = (s0, s1, s2, s3)
    top_part, peak = (top_part0, top_part1), (peak0, peak1)
    depth = q_ref.shape[1]
    gain = 3.0 / math.sqrt(depth) * LOG2E
    local_e = ex.shape[0]
    chunks = local_e // WIDE
    tiles = WIDE // 128
    g = lax.axis_index("grp")
    me = lax.axis_index("idx")
    x, z, y = me // (Z * Y), (me // Y) % Z, me % Y

    def place(dx, dz, y_at):
        return (g, lax.rem(x + dx + X, X) * (Z * Y) + lax.rem(z + dz + Z, Z) * Y + y_at)

    near = {
        "xp": place(1, 0, y), "xm": place(-1, 0, y), "zp": place(0, 1, y), "zm": place(0, -1, y),
    }
    partner = place(0, 0, 1 - y)
    peers = [(lax.rem(g + k, groups), me) for k in range(1, groups)]

    loads = [
        pltpu.make_async_copy(
            ex_hbm.at[pl.ds(n * WIDE, WIDE)], ex.at[pl.ds(n * WIDE, WIDE)], load_sem.at[n]
        )
        for n in range(chunks)
    ]
    label_load = pltpu.make_async_copy(labels_hbm, labels_raw, load_sem.at[chunks])
    label_load.start()
    for load in loads:
        load.start()

    barrier = pltpu.get_barrier_semaphore()
    greeted = [partner, *peers]
    greeted += [place(dx, 0, side) for dx in X_ORDER[1:] for side in (0, 1)]
    greeted += [place(0, dz, y) for dz in Z_ORDER[1:]]
    for other in greeted:
        pl.semaphore_signal(barrier, inc=1, device_id=other, device_id_type=MESH)
    pl.semaphore_wait(barrier, len(greeted))

    def move(name):
        source, count, target, way = MOVES[name]
        sem = MOVE_IDS[name]
        return pltpu.make_async_remote_copy(
            src_ref=rows.at[pl.ds(source, count * SHARD)],
            dst_ref=rows.at[pl.ds(target, count * SHARD)],
            send_sem=send.at[sem], recv_sem=recv.at[sem],
            device_id=near[way], device_id_type=MESH,
        )

    def go(*names):
        for name in names:
            move(name).start()

    def got(*names):
        for name in names:
            move(name).wait_recv()

    def cross(at):
        return pltpu.make_async_remote_copy(
            src_ref=q_ref, dst_ref=rows.at[pl.ds(pl.multiple_of(at, SHARD), SHARD)],
            send_sem=send.at[0], recv_sem=recv.at[0], device_id=partner, device_id_type=MESH,
        )

    own_row = y * row_of(1, 0, 0)
    cross(own_row).start()
    rows[pl.ds(pl.multiple_of(own_row, SHARD), SHARD), :] = q_ref[...]

    label_load.wait()
    rest = lax.broadcasted_iota(jnp.int32, (128 - CATEGORIES, WIDE), 0) + CATEGORIES
    for n in range(chunks):
        at = pl.ds(n * WIDE, WIDE)
        labels[0:CATEGORIES, at] = labels_raw[:, at].astype(jnp.float32).astype(jnp.bfloat16)
        labels[CATEGORIES:128, at] = jnp.where(rest == MASS, 1.0, 0.0).astype(jnp.bfloat16)
    row_sum[...] = jnp.zeros_like(row_sum)
    col_max[...] = jnp.full_like(col_max, LOWEST)
    col_sum[...] = jnp.zeros_like(col_sum)

    cross((1 - y) * row_of(1, 0, 0)).wait_recv()
    go("x+", "x-", ("w+", 1), ("w-", 1), ("v+", 0), ("v-", 0))
    got("x+", "x-")
    go("x2", ("z+", 1, 0), ("z-", 1, 0))
    got(("w+", 1), ("w-", 1))
    go(("w+", 2), ("w-", 2), ("v+", 1), ("v-", 1))
    got("x2")
    go(("z+", 1, 1), ("z-", 1, 1))
    got(("w+", 2), ("w-", 2))
    go(("w+", 3), ("w-", 3), ("v+", 2), ("v-", 2))
    got(("z+", 1, 0), ("z-", 1, 0))
    go(("z+", 2, 0), ("z-", 2, 0))
    got(("w+", 3), ("w-", 3))
    go(("w+", 4), ("v+", 3), ("v-", 3))
    got(("z+", 1, 1), ("z-", 1, 1))
    go(("z+", 2, 1), ("z-", 2, 1))

    def event(at):
        if at == (0, 1):
            got(("w+", 4))
            go(("v+", 4), ("v-", 4))
            got(("v+", 0), ("v-", 0), ("v+", 1), ("v-", 1))
            go(("u+", 0), ("u+", 1))
        if at == (0, 2):
            got(("v+", 2), ("v-", 2))
            go(("u-", 2))
            got(("z+", 2, 0), ("z-", 2, 0))
            go(("z+", 3, 0), ("z-", 3, 0))
        if at == (0, 3):
            got(("v+", 3), ("v-", 3))
            go(("u-", 3))
        if at == (1, 0):
            got(("z+", 2, 1), ("z-", 2, 1))
            go(("z+", 3, 1), ("z-", 3, 1))
            got(("v+", 4), ("v-", 4))
            go(("u+", 4))
        if at == (1, 2):
            got(("z+", 3, 0), ("z-", 3, 0))
            go(("z+", 4, 0))
        if at == (2, 0):
            got(("u+", 0), ("u+", 1), ("u-", 2))
            got(("z+", 3, 1), ("z-", 3, 1))
            go(("z-", 4, 1))
        if at == (3, 0):
            got(("u-", 3), ("u+", 4), ("z+", 4, 0), ("z-", 4, 1))

    def score(b, n):
        at = pl.ds(n * WIDE, WIDE)
        s = dot_t(rows[pl.ds(b * BLOCK, BLOCK), :], ex[at, :]) * gain
        scores[b][:, at] = s
        top = s[:, 0:128]
        for t in range(1, tiles):
            top = jnp.maximum(top, s[:, t * 128 : (t + 1) * 128])
        ref = top_part[b % 2]
        ref[...] = top if n == 0 else jnp.maximum(ref[...], top)
        peak[b % 2][:, at] = jnp.max(s.reshape(BLOCK // 8, 8, WIDE), axis=0)

    def total(b, n, tall=32, wide=512):
        at = pl.ds(n * WIDE, WIDE)
        old = col_max[:, at]
        new = jnp.maximum(old, peak[b % 2][:, at])
        col_max[:, at] = new
        scaled = col_sum[:, at] * jnp.exp2(old - new)
        for c in range(0, WIDE, wide):
            shift = new[:, c : c + wide]
            col = scaled[:, c : c + wide]
            for r in range(0, BLOCK, tall):
                s = scores[b][r : r + tall, n * WIDE + c : n * WIDE + c + wide]
                col = col + jnp.exp2(s.reshape(tall // 8, 8, wide) - shift[None]).sum(0)
                mine = pl.ds(b * BLOCK + r, tall)
                top = row_top[mine, :]
                row = row_sum[mine, :]
                for u in range(0, wide, 128):
                    row = row + jnp.exp2(s[:, u : u + 128] - top)
                row_sum[mine, :] = row
            col_sum[:, n * WIDE + c : n * WIDE + c + wide] = col

    def hub_move(k, n):
        at = pl.ds(n * tiles, tiles)
        return pltpu.make_async_remote_copy(
            src_ref=hubs.at[0, at], dst_ref=hubs.at[k, at],
            send_sem=hub_send.at[k, n], recv_sem=hub_recv.at[k, n],
            device_id=peers[k - 1], device_id_type=MESH,
        )

    def hub_part(n):
        at = pl.ds(n * WIDE, WIDE)
        top = jnp.max(col_max[:, at], axis=0, keepdims=True)
        whole = jnp.sum(col_sum[:, at] * jnp.exp2(col_max[:, at] - top), axis=0, keepdims=True)
        lse = top + jnp.log(whole) * LOG2E
        for t in range(tiles):
            hubs[0, n * tiles + t : n * tiles + t + 1, :] = lse[:, t * 128 : (t + 1) * 128]
        for k in range(1, groups):
            hub_move(k, n).start()

    blocks = len(scores)
    for b in range(blocks + 1):
        for n in range(chunks):
            event((b, n))
            if b < blocks:
                if b == 0:
                    loads[n].wait()
                score(b, n)
            if b > 0:
                total(b - 1, n)
            if b == blocks:
                hub_part(n)
        if b < blocks:
            row_top[pl.ds(b * BLOCK, BLOCK), :] = jnp.broadcast_to(
                jnp.max(top_part[b % 2][...], axis=1, keepdims=True), (BLOCK, 128)
            )

    for k in range(1, groups):
        for n in range(chunks):
            hub_move(k, n).wait_recv()
    parts = [hubs[k] for k in range(groups)]
    top = functools.reduce(jnp.maximum, parts)
    whole = sum(jnp.exp2(part - top) for part in parts)
    half_hub = 0.5 * (top + jnp.log(whole) * LOG2E - math.log2(total_q))
    for t in range(local_e // 128):
        hub_row[:, t * 128 : (t + 1) * 128] = half_hub[t : t + 1, :]

    wide_lane = lax.broadcasted_iota(jnp.int32, (BLOCK, 128), 1)
    half = local_e // 2

    def weigh(b):
        ref = scores[b]
        best = jnp.full((BLOCK, 128), LOWEST, jnp.float32)
        for t in range(local_e // 128):
            at = slice(t * 128, (t + 1) * 128)
            best = jnp.maximum(best, ref[:, at] - hub_row[0:1, at])
        top = jnp.max(best, axis=1, keepdims=True)
        acc = jnp.zeros((BLOCK, 128), jnp.float32)
        for c in range(0, local_e, half):
            at = slice(c, c + half)
            over = ref[:, at] - hub_row[0:1, at] - top
            weights = jnp.exp2(over + over).astype(jnp.bfloat16)
            acc = acc + dot_t(weights, labels[:, at])
        mine = pl.ds(b * BLOCK, BLOCK)
        dens = row_top[mine, :] + LOG2E * jnp.log(
            jnp.sum(row_sum[mine, :], axis=1, keepdims=True)
        )
        numer[mine, :] = jnp.where(
            wide_lane == TOP, top, jnp.where(wide_lane == DENS, dens, acc)
        )

    def pack(side, dx):
        if side == 1:
            part = numer[SECOND_BASE[dx] : SECOND_BASE[dx] + 128, :]
        else:
            starts = [row_of(0, dx, dz) for dz in Z_ORDER]
            part = jnp.concatenate([numer[r : r + SHARD, :] for r in starts], axis=0)
        packed[2 * X_ORDER.index(dx) + side] = part.T[0:PACKED, :]

    def a_move(slot, to):
        return pltpu.make_async_remote_copy(
            src_ref=packed.at[slot], dst_ref=arrived.at[slot - slot % 2 + y],
            send_sem=a_send.at[slot], recv_sem=a_recv.at[slot - slot % 2 + y],
            device_id=to, device_id_type=MESH,
        )

    def a_wait(slot):
        pltpu.make_async_remote_copy(
            src_ref=arrived.at[slot], dst_ref=arrived.at[slot],
            send_sem=a_send.at[slot], recv_sem=a_recv.at[slot],
            device_id=partner, device_id_type=MESH,
        ).wait_recv()

    def deliver(dx, side):
        pack(side, dx)
        slot = 2 * X_ORDER.index(dx) + side
        a_move(slot, place(dx, 0, side)).start()

    weigh(0)
    weigh(1)
    pack(1, 0)
    deliver(1, 1)
    weigh(2)
    deliver(-1, 1)
    weigh(3)
    deliver(2, 1)
    for dx in (2, 1, -1):
        deliver(dx, 0)
    pack(0, 0)
    a_move(1 - y, partner).start()
    arrived[y] = packed[y]

    a_wait(1 - y)
    for slot in range(2, 2 * X):
        a_wait(slot)
    parts = [arrived[k] for k in range(2 * X)]
    tops = [part[TOP : TOP + 1, :] for part in parts]
    dens = [part[DENS : DENS + 1, :] for part in parts]
    top = functools.reduce(jnp.maximum, tops)
    summed = jnp.zeros((PACKED, 128), jnp.float32)
    for part, mine in zip(parts, tops):
        over = mine - top
        summed = summed + part * jnp.exp2(over + over)
    dens_top = functools.reduce(jnp.maximum, dens)
    dens_sum = sum(jnp.exp2(mine - dens_top) for mine in dens)
    dens_lse = dens_top + jnp.log(dens_sum) * LOG2E
    place_row = lax.broadcasted_iota(jnp.int32, (PACKED, 128), 0)
    summed = jnp.where(place_row == TOP, top, jnp.where(place_row == DENS, dens_lse, summed))
    full = jnp.concatenate([summed, jnp.zeros((128 - PACKED, 128), jnp.float32)], axis=0)
    spread[...] = full.T

    def b_move(k):
        return pltpu.make_async_remote_copy(
            src_ref=spread.at[pl.ds(k * SHARD, SHARD)], dst_ref=last.at[k],
            send_sem=b_send.at[k], recv_sem=b_recv.at[k],
            device_id=place(0, Z_ORDER[k], y), device_id_type=MESH,
        )

    for k in (7, 6, 5, 4, 3, 2, 1):
        b_move(k).start()
    last[0] = spread[0:SHARD, :]
    for k in range(1, Z):
        b_move(k).wait_recv()
    parts = [last[k] for k in range(Z)]
    tops = [part[:, TOP : TOP + 1] for part in parts]
    dens = [part[:, DENS : DENS + 1] for part in parts]
    top = functools.reduce(jnp.maximum, tops)
    summed = jnp.zeros((SHARD, 128), jnp.float32)
    for part, mine in zip(parts, tops):
        over = mine - top
        summed = summed + part * jnp.exp2(over + over)
    risk_ref[...] = summed[:, 0:CATEGORIES] / summed[:, MASS : MASS + 1]
    dens_top = functools.reduce(jnp.maximum, dens)
    dens_sum = sum(jnp.exp2(mine - dens_top) for mine in dens)
    density = dens_top / LOG2E + jnp.log(dens_sum) - math.log(total_e)
    density_ref[...] = jnp.broadcast_to(density, (SHARD, 128)).T[0:1, 0:SHARD]

    cross(own_row).wait_send()
    for name in MOVES:
        move(name).wait_send()
    for k in range(1, groups):
        for n in range(chunks):
            hub_move(k, n).wait_send()
    for slot in range(2, 2 * X):
        a_move(slot, partner).wait_send()
    a_move(1 - y, partner).wait_send()
    for k in range(1, Z):
        b_move(k).wait_send()


def per_device(queries, exemplars, labels):
    groups = lax.axis_size("grp")
    devices = lax.axis_size("idx")
    local_q, depth = queries.shape
    local_e = exemplars.shape[0]
    group_q = local_q * devices
    f32, bf16 = jnp.float32, jnp.bfloat16
    vmem, dma = pltpu.VMEM, pltpu.SemaphoreType.DMA
    chunks = local_e // WIDE
    here = pl.BlockSpec(memory_space=pltpu.VMEM)
    away = pl.BlockSpec(memory_space=pl.ANY)
    risk, density = pl.pallas_call(
        functools.partial(kernel, groups, group_q * groups, local_e * devices),
        out_shape=(
            jax.ShapeDtypeStruct((local_q, CATEGORIES), f32),
            jax.ShapeDtypeStruct((1, local_q), f32),
        ),
        in_specs=[here, away, away],
        out_specs=(here, here),
        scratch_shapes=[
            vmem((group_q, depth), bf16),
            vmem((local_e, depth), bf16),
            vmem((CATEGORIES, local_e), jnp.int32),
            vmem((128, local_e), bf16),
            *[vmem((BLOCK, local_e), f32)] * 4,
            *[vmem((BLOCK, 128), f32)] * 2,
            *[vmem((group_q, 128), f32)] * 2,
            *[vmem((8, local_e), f32)] * 4,
            vmem((groups, local_e // 128, 128), f32),
            vmem((1, local_e), f32),
            vmem((group_q, 128), f32),
            vmem((2 * X, PACKED, 128), f32),
            vmem((2 * X, PACKED, 128), f32),
            vmem((128, 128), f32),
            vmem((Z, SHARD, 128), f32),
            dma((chunks + 1,)),
            dma((N_MOVES,)),
            dma((N_MOVES,)),
            dma((groups, chunks)),
            dma((groups, chunks)),
            dma((2 * X,)),
            dma((2 * X,)),
            dma((Z,)),
            dma((Z,)),
        ],
        compiler_params=pltpu.CompilerParams(
            collective_id=0, has_side_effects=True, vmem_limit_bytes=58 * 2**20
        ),
        cost_estimate=pl.CostEstimate(
            flops=2 * group_q * local_e * (depth + 128),
            bytes_accessed=local_e * depth * 2 + local_e * CATEGORIES * 4,
            transcendentals=3 * group_q * local_e,
        ),
        name="prefilter",
    )(queries, exemplars, labels.T)
    return risk, density.reshape(local_q)


def solution(mesh):
    in_specs = (P(("grp", "idx"), None), P("idx", None), P("idx", None))
    out_specs = (P(("grp", "idx"), None), P(("grp", "idx")))
    return jax.shard_map(
        per_device, mesh=mesh, in_specs=in_specs, out_specs=out_specs, check_vma=False
    )
```

```python
import functools
import math

import jax
import jax.numpy as jnp
from jax import lax
from jax.experimental import pallas as pl
from jax.experimental.pallas import tpu as pltpu
from jax.sharding import PartitionSpec as P

X, Z, Y, GROUPS = 4, 8, 2, 4
SHARD = 16
X_ORDER = (0, 1, -1, 2)
Z_ORDER = (0, 1, -1, 2, -2, 3, -3, 4)
FIRST_BASE = {0: 0, 1: 64, -1: 128, 2: 256, -2: 320, 3: 768, -3: 832, 4: 896}
NEAR_BASE = {0: 192, 1: 384, -1: 448, 2: 704}
FAR_BASE = {0: 512, 1: 576, -1: 640, 2: 960}
PIECES = ((0, 1), (1, 2), (2, 1), (-2, 1), (3, 2), (4, 1))
BLOCK = 256
WIDE = 1024
CATEGORIES = 64
MASS, TOP, DENS, UNUSED = 64, 67, 70, 73
LOG2E = 1.4426950408889634
LOWEST = -1e30
MESH = pl.DeviceIdType.MESH


def row_of(side, dx, dz):
    if side == 0:
        return FIRST_BASE[dz] + SHARD * X_ORDER.index(dx)
    at = Z_ORDER.index(dz)
    return NEAR_BASE[dx] + SHARD * at if at < 4 else FAR_BASE[dx] + SHARD * (at - 4)


def gather_moves():
    moves = {}
    for k in (1, 2, 3, 4):
        far = 4 if k == 4 else -k
        for half in (0, 1):
            off = 32 * half
            if k < 4 or half == 0:
                moves["z+", k, half] = (FIRST_BASE[1 - k] + off, 2, FIRST_BASE[far] + off, "zp")
            if k < 4 or half == 1:
                moves["z-", k, half] = (FIRST_BASE[k - 1] + off, 2, FIRST_BASE[k] + off, "zm")
    for g, (dz, count) in enumerate(PIECES):
        own = row_of(1, 0, dz)
        moves["v+", g] = (own, count, row_of(1, -1, dz), "xp")
        moves["v-", g] = (own, count, row_of(1, 1, dz), "xm")
        if g in (0, 1, 5):
            moves["u+", g] = (row_of(1, -1, dz), count, row_of(1, 2, dz), "xp")
        else:
            moves["u-", g] = (row_of(1, 1, dz), count, row_of(1, 2, dz), "xm")
    moves["w+", 3] = (row_of(1, 0, -2), 1, row_of(1, 0, -3), "zp")
    moves["w-", 3] = (row_of(1, 0, 2), 1, row_of(1, 0, 3), "zm")
    moves["w+", 4] = (row_of(1, 0, -2), 1, row_of(1, 0, 4), "zpp")
    for g, (dz, count) in enumerate(PIECES):
        if g > 0:
            moves["f", g] = (row_of(1, 0, dz), count, row_of(1, 0, dz), "partner")
    return moves


MOVES = gather_moves()
EVERY_MOVES = [name for name in MOVES if name[0][0] in "zvu"]
FOUND_MOVES = [name for name in MOVES if name[0] in ("w+", "w-")]
HANDED_MOVES = [name for name in MOVES if name[0] == "f"]
MOVE_IDS = {name: i for i, name in enumerate(MOVES)}
FIRST_WAY = {(0, dx): len(MOVES) + i for i, dx in enumerate(X_ORDER)}
SECOND_WAY = {dz: len(MOVES) + len(X_ORDER) + i for i, dz in enumerate(Z_ORDER[0:5])}
N_MOVES = len(MOVES) + len(X_ORDER) + 5
SENDERS = X * Z * Y


def dot_t(a, b):
    return lax.dot_general(a, b, (((1,), (1,)), ((), ())), preferred_element_type=jnp.float32)


def kernel(
    groups, total_q, total_e,
    q_ref, ex_hbm, labels_hbm, risk_ref, density_ref,
    rows, ex, labels_raw, labels, s0, s1, s2, s3,
    top_part0, top_part1, row_top, row_sum, peak0, peak1, col_max, col_sum,
    best, hubs, hub_row, numer, arrived,
    load_sem, send, recv, own_send, hub_send, hub_recv, sum_send, sum_recv,
):
    scores = (s0, s1, s2, s3)
    top_part, peak = (top_part0, top_part1), (peak0, peak1)
    depth = q_ref.shape[1]
    gain = 3.0 / math.sqrt(depth) * LOG2E
    local_e = ex.shape[0]
    chunks = local_e // WIDE
    tiles = WIDE // 128
    g = lax.axis_index("grp")
    me = lax.axis_index("idx")
    x, z, y = me // (Z * Y), (me // Y) % Z, me % Y

    def place(dx, dz, y_at):
        return (g, lax.rem(x + dx + X, X) * (Z * Y) + lax.rem(z + dz + Z, Z) * Y + y_at)

    near = {
        "xp": place(1, 0, y), "xm": place(-1, 0, y), "zp": place(0, 1, y), "zm": place(0, -1, y),
        "zpp": place(0, 2, y), "partner": place(0, 0, 1 - y),
    }
    partner = near["partner"]
    peers = [(lax.rem(g + k, groups), me) for k in range(1, groups)]

    loads = [
        pltpu.make_async_copy(
            ex_hbm.at[pl.ds(n * WIDE, WIDE)], ex.at[pl.ds(n * WIDE, WIDE)], load_sem.at[n]
        )
        for n in range(chunks)
    ]
    label_load = pltpu.make_async_copy(labels_hbm, labels_raw, load_sem.at[chunks])
    label_load.start()
    for load in loads:
        load.start()

    barrier = pltpu.get_barrier_semaphore()
    greeted = [partner, *peers]
    greeted += [place(dx, 0, side) for dx in X_ORDER[1:] for side in (0, 1)]
    greeted += [place(0, dz, y) for dz in Z_ORDER[1:5]]
    for other in greeted:
        pl.semaphore_signal(barrier, inc=1, device_id=other, device_id_type=MESH)
    pl.semaphore_wait(barrier, len(greeted))

    def move(name):
        source, count, target, way = MOVES[name]
        sem = MOVE_IDS[name]
        return pltpu.make_async_remote_copy(
            src_ref=rows.at[pl.ds(source, count * SHARD)],
            dst_ref=rows.at[pl.ds(target, count * SHARD)],
            send_sem=send.at[sem], recv_sem=recv.at[sem],
            device_id=near[way], device_id_type=MESH,
        )

    def go(*names):
        for name in names:
            move(name).start()

    def got(*names):
        for name in names:
            move(name).wait_recv()

    def away(k, target, sem, to):
        return pltpu.make_async_remote_copy(
            src_ref=q_ref, dst_ref=rows.at[pl.ds(target, SHARD)],
            send_sem=own_send.at[k], recv_sem=recv.at[sem], device_id=to, device_id_type=MESH,
        )

    first_away = [away(0, row_of(0, 0, 0), FIRST_WAY[0, 0], partner)]
    for dx in X_ORDER[1:]:
        back = dx if dx == 2 else -dx
        for side in (0, 1):
            first_away.append(
                away(
                    len(first_away), row_of(0, back, 0), FIRST_WAY[0, back], place(dx, 0, side)
                )
            )
    second_away = [away(0, row_of(1, 0, 0), SECOND_WAY[0], partner)]
    for dz in Z_ORDER[1:5]:
        second_away.append(
            away(len(second_away), row_of(1, 0, -dz), SECOND_WAY[-dz], place(0, dz, y))
        )

    def landed(target, sem):
        away(0, target, sem, partner).wait_recv()

    @pl.when(y == 0)
    def _():
        for copy in first_away:
            copy.start()

    @pl.when(y == 1)
    def _():
        for copy in second_away:
            copy.start()

    own_row = y * row_of(1, 0, 0)
    rows[pl.ds(pl.multiple_of(own_row, SHARD), SHARD), :] = q_ref[...]

    label_load.wait()
    rest = lax.broadcasted_iota(jnp.int32, (128 - CATEGORIES, WIDE), 0) + CATEGORIES
    for n in range(chunks):
        at = pl.ds(n * WIDE, WIDE)
        labels[0:CATEGORIES, at] = labels_raw[:, at].astype(jnp.float32).astype(jnp.bfloat16)
        labels[CATEGORIES:128, at] = jnp.where(rest == MASS, 1.0, 0.0).astype(jnp.bfloat16)
    row_sum[...] = jnp.zeros_like(row_sum)
    col_max[...] = jnp.full_like(col_max, LOWEST)
    col_sum[...] = jnp.zeros_like(col_sum)

    @pl.when(y == 0)
    def _():
        landed(row_of(1, 0, 0), SECOND_WAY[0])

    go(("v+", 0), ("v-", 0))

    @pl.when(y == 1)
    def _():
        landed(row_of(0, 0, 0), FIRST_WAY[0, 0])
        landed(row_of(1, 0, 1), SECOND_WAY[1])
        landed(row_of(1, 0, -1), SECOND_WAY[-1])
        go(("f", 1), ("v+", 1), ("v-", 1))
        landed(row_of(1, 0, 2), SECOND_WAY[2])
        go(("f", 2), ("w-", 3), ("v+", 2), ("v-", 2))
        landed(row_of(1, 0, -2), SECOND_WAY[-2])
        go(("f", 3), ("w+", 3), ("w+", 4), ("v+", 3), ("v-", 3))

    for dx in X_ORDER[1:]:
        landed(row_of(0, dx, 0), FIRST_WAY[0, dx])
    go(("z+", 1, 0), ("z-", 1, 0), ("z+", 1, 1), ("z-", 1, 1))

    @pl.when(y == 0)
    def _():
        for g in (1, 2, 3):
            got(("f", g))
            go(("v+", g), ("v-", g))

    for half in (0, 1):
        got(("z+", 1, half), ("z-", 1, half))
        go(("z+", 2, half), ("z-", 2, half))

    def event(at):
        if at == (0, 1):
            got(("v+", 0), ("v-", 0))
            go(("u+", 0))
        if at == (0, 2):

            @pl.when(y == 1)
            def _():
                got(("w+", 3), ("w-", 3))
                go(("f", 4), ("v+", 4), ("v-", 4))
                got(("w+", 4))
                go(("f", 5), ("v+", 5), ("v-", 5))

        if at == (0, 3):
            got(("v+", 1), ("v-", 1))
            go(("u+", 1))
            got(("v+", 2), ("v-", 2))
            go(("u-", 2))
            got(("v+", 3), ("v-", 3))
            go(("u-", 3))
        if at == (1, 0):
            for half in (0, 1):
                got(("z+", 2, half), ("z-", 2, half))
                go(("z+", 3, half), ("z-", 3, half))
        if at == (1, 1):

            @pl.when(y == 0)
            def _():
                for g in (4, 5):
                    got(("f", g))
                    go(("v+", g), ("v-", g))

        if at == (1, 3):
            got(("z+", 3, 0), ("z-", 3, 0))
            go(("z+", 4, 0))
        if at == (2, 0):
            got(("z+", 3, 1), ("z-", 3, 1))
            go(("z-", 4, 1))
            got(("v+", 4), ("v-", 4))
            go(("u-", 4))
            got(("v+", 5), ("v-", 5))
            go(("u+", 5))
            got(("u+", 0), ("u+", 1), ("u-", 2))
        if at == (3, 0):
            got(("z+", 4, 0), ("z-", 4, 1), ("u-", 3), ("u-", 4), ("u+", 5))

    def score(b, n):
        at = pl.ds(n * WIDE, WIDE)
        s = dot_t(rows[pl.ds(b * BLOCK, BLOCK), :], ex[at, :]) * gain
        scores[b][:, at] = s
        top = s[:, 0:128]
        for t in range(1, tiles):
            top = jnp.maximum(top, s[:, t * 128 : (t + 1) * 128])
        ref = top_part[b % 2]
        ref[...] = top if n == 0 else jnp.maximum(ref[...], top)
        peak[b % 2][:, at] = jnp.max(s.reshape(BLOCK // 8, 8, WIDE), axis=0)

    def total(b, n, rowwise=True, colwise=True, tall=32, wide=512):
        at = pl.ds(n * WIDE, WIDE)
        if colwise:
            old = col_max[:, at]
            new = jnp.maximum(old, peak[b % 2][:, at])
            col_max[:, at] = new
            scaled = col_sum[:, at] * jnp.exp2(old - new)
        for c in range(0, WIDE, wide):
            if colwise:
                shift = new[:, c : c + wide]
                col = scaled[:, c : c + wide]
            for r in range(0, BLOCK, tall):
                s = scores[b][r : r + tall, n * WIDE + c : n * WIDE + c + wide]
                if colwise:
                    col = col + jnp.exp2(s.reshape(tall // 8, 8, wide) - shift[None]).sum(0)
                if rowwise:
                    mine = pl.ds(b * BLOCK + r, tall)
                    top = row_top[mine, :]
                    row = row_sum[mine, :]
                    for u in range(0, wide, 128):
                        row = row + jnp.exp2(s[:, u : u + 128] - top)
                    row_sum[mine, :] = row
            if colwise:
                col_sum[:, n * WIDE + c : n * WIDE + c + wide] = col

    def hub_move(k, n):
        at = pl.ds(n * tiles, tiles)
        return pltpu.make_async_remote_copy(
            src_ref=hubs.at[0, at], dst_ref=hubs.at[k, at],
            send_sem=hub_send.at[k, n], recv_sem=hub_recv.at[k, n],
            device_id=peers[k - 1], device_id_type=MESH,
        )

    def hub_part(n):
        at = pl.ds(n * WIDE, WIDE)
        top = jnp.max(col_max[:, at], axis=0, keepdims=True)
        whole = jnp.sum(col_sum[:, at] * jnp.exp2(col_max[:, at] - top), axis=0, keepdims=True)
        lse = top + jnp.log(whole) * LOG2E
        for t in range(tiles):
            hubs[0, n * tiles + t : n * tiles + t + 1, :] = lse[:, t * 128 : (t + 1) * 128]
        for k in range(1, groups):
            hub_move(k, n).start()

    blocks = len(scores)
    final = blocks - 1
    for b in range(blocks):
        for n in range(chunks):
            event((b, n))
            if b == 0:
                loads[n].wait()
            score(b, n)
            if b > 0:
                total(b - 1, n)
            if b == final:
                total(b, n, rowwise=False)
                hub_part(n)
        row_top[pl.ds(b * BLOCK, BLOCK), :] = jnp.broadcast_to(
            jnp.max(top_part[b % 2][...], axis=1, keepdims=True), (BLOCK, 128)
        )
    for n in range(chunks):
        total(final, n, colwise=False)

    for n in range(chunks):
        at = pl.ds(n * tiles, tiles)
        for k in range(1, groups):
            hub_move(k, n).wait_recv()
        parts = [hubs[k, at] for k in range(groups)]
        top = functools.reduce(jnp.maximum, parts)
        whole = sum(jnp.exp2(part - top) for part in parts)
        half_hub = 0.5 * (top + jnp.log(whole) * LOG2E - math.log2(total_q))
        for t in range(tiles):
            hub_row[:, n * WIDE + t * 128 : n * WIDE + (t + 1) * 128] = half_hub[t : t + 1, :]
        for b in range(blocks):
            mine = pl.ds(b * BLOCK, BLOCK)
            top = scores[b][:, n * WIDE : n * WIDE + 128] - hub_row[:, n * WIDE : n * WIDE + 128]
            for t in range(1, tiles):
                at_t = slice(n * WIDE + t * 128, n * WIDE + (t + 1) * 128)
                top = jnp.maximum(top, scores[b][:, at_t] - hub_row[:, at_t])
            best[mine, :] = top if n == 0 else jnp.maximum(best[mine, :], top)

    wide_lane = lax.broadcasted_iota(jnp.int32, (BLOCK, 128), 1)
    half = local_e // 2

    def weigh(b):
        ref = scores[b]
        mine = pl.ds(b * BLOCK, BLOCK)
        top = jnp.max(best[mine, :], axis=1, keepdims=True)
        acc = jnp.zeros((BLOCK, 128), jnp.float32)
        for c in range(0, local_e, half):
            at = slice(c, c + half)
            over = ref[:, at] - hub_row[0:1, at] - top
            weights = jnp.exp2(over + over).astype(jnp.bfloat16)
            acc = acc + dot_t(weights, labels[:, at])
        dens = row_top[mine, :] + LOG2E * jnp.log(
            jnp.sum(row_sum[mine, :], axis=1, keepdims=True)
        )
        figure = jnp.where(
            wide_lane < TOP, acc[:, MASS : MASS + 1], jnp.where(wide_lane < DENS, top, dens)
        )
        high = figure.astype(jnp.bfloat16).astype(jnp.float32)
        middle = (figure - high).astype(jnp.bfloat16).astype(jnp.float32)
        low = figure - high - middle
        turn = lax.rem(wide_lane - MASS, 3)
        piece = jnp.where(turn == 0, high, jnp.where(turn == 1, middle, low))
        piece = jnp.where(wide_lane < UNUSED, piece, 0.0)
        numer[mine, :] = jnp.where(wide_lane < MASS, acc, piece).astype(jnp.bfloat16)

    def slot_of(side, dx, dz):
        return (side * X + X_ORDER.index(dx)) * Z + Z_ORDER.index(dz)

    def sum_move(source, sender, slot, to):
        return pltpu.make_async_remote_copy(
            src_ref=numer.at[pl.ds(source, SHARD)], dst_ref=arrived.at[slot],
            send_sem=sum_send.at[sender], recv_sem=sum_recv.at[slot],
            device_id=to, device_id_type=MESH,
        )

    others = [
        (side, dx, dz)
        for dz in reversed(Z_ORDER)
        for dx in reversed(X_ORDER)
        for side in (0, 1)
        if (dx, dz) != (0, 0)
    ]

    def hand_out(side, dx, dz):
        return sum_move(
            row_of(side, dx, dz), slot_of(side, dx, dz), slot_of(0, dx, dz) + y * (X * Z),
            place(dx, dz, side),
        )

    partner_row = pl.multiple_of((1 - y) * row_of(1, 0, 0), SHARD)
    hand_partner = sum_move(partner_row, 0, y * (X * Z), partner)
    for b in reversed(range(blocks)):
        weigh(b)
        for where in others:
            if row_of(*where) // BLOCK == b:
                hand_out(*where).start()
    hand_partner.start()
    arrived[y * (X * Z)] = numer[pl.ds(pl.multiple_of(own_row, SHARD), SHARD), :]

    for where in others:
        sum_move(0, slot_of(*where), slot_of(*where), partner).wait_recv()
    sum_move(0, 0, (1 - y) * (X * Z), partner).wait_recv()

    parts = arrived[...].astype(jnp.float32)
    lane = lax.broadcasted_iota(jnp.int32, parts.shape, 2)

    def figure_of(first):
        inside = (lane >= first) & (lane < first + 3)
        return jnp.sum(jnp.where(inside, parts, 0.0), axis=2, keepdims=True)

    tops, dens = figure_of(TOP), figure_of(DENS)
    over = tops - jnp.max(tops, axis=0, keepdims=True)
    summed = jnp.sum(parts * jnp.exp2(over + over), axis=0)
    mass = summed[:, MASS : MASS + 1] + summed[:, MASS + 1 : MASS + 2]
    mass = mass + summed[:, MASS + 2 : MASS + 3]
    risk_ref[...] = summed[:, 0:CATEGORIES] / mass
    dens_top = jnp.max(dens, axis=0, keepdims=True)
    dens_sum = jnp.sum(jnp.exp2(dens - dens_top), axis=0)
    density = dens_top[0] / LOG2E + jnp.log(dens_sum) - math.log(total_e)
    density_ref[...] = jnp.broadcast_to(density, (SHARD, 128)).T[0:1, 0:SHARD]

    @pl.when(y == 0)
    def _():
        for copy in first_away:
            copy.wait_send()

    @pl.when(y == 1)
    def _():
        for copy in second_away:
            copy.wait_send()
        for name in FOUND_MOVES + HANDED_MOVES:
            move(name).wait_send()

    for name in EVERY_MOVES:
        move(name).wait_send()
    for k in range(1, groups):
        for n in range(chunks):
            hub_move(k, n).wait_send()
    for where in others:
        hand_out(*where).wait_send()
    hand_partner.wait_send()


def per_device(queries, exemplars, labels):
    groups = lax.axis_size("grp")
    devices = lax.axis_size("idx")
    local_q, depth = queries.shape
    local_e = exemplars.shape[0]
    group_q = local_q * devices
    f32, bf16 = jnp.float32, jnp.bfloat16
    vmem, dma = pltpu.VMEM, pltpu.SemaphoreType.DMA
    chunks = local_e // WIDE
    here = pl.BlockSpec(memory_space=pltpu.VMEM)
    away = pl.BlockSpec(memory_space=pl.ANY)
    risk, density = pl.pallas_call(
        functools.partial(kernel, groups, group_q * groups, local_e * devices),
        out_shape=(
            jax.ShapeDtypeStruct((local_q, CATEGORIES), f32),
            jax.ShapeDtypeStruct((1, local_q), f32),
        ),
        in_specs=[here, away, away],
        out_specs=(here, here),
        scratch_shapes=[
            vmem((group_q, depth), bf16),
            vmem((local_e, depth), bf16),
            vmem((CATEGORIES, local_e), jnp.int32),
            vmem((128, local_e), bf16),
            *[vmem((BLOCK, local_e), f32)] * 4,
            *[vmem((BLOCK, 128), f32)] * 2,
            *[vmem((group_q, 128), f32)] * 2,
            *[vmem((8, local_e), f32)] * 4,
            vmem((group_q, 128), f32),
            vmem((groups, local_e // 128, 128), f32),
            vmem((1, local_e), f32),
            vmem((group_q, 128), bf16),
            vmem((SENDERS, SHARD, 128), bf16),
            dma((chunks + 1,)),
            dma((N_MOVES,)),
            dma((N_MOVES,)),
            dma((2 * X - 1,)),
            dma((groups, chunks)),
            dma((groups, chunks)),
            dma((SENDERS,)),
            dma((SENDERS,)),
        ],
        compiler_params=pltpu.CompilerParams(
            collective_id=0, has_side_effects=True, vmem_limit_bytes=58 * 2**20
        ),
        cost_estimate=pl.CostEstimate(
            flops=2 * group_q * local_e * (depth + 128),
            bytes_accessed=local_e * depth * 2 + local_e * CATEGORIES * 4,
            transcendentals=3 * group_q * local_e,
        ),
        name="prefilter",
    )(queries, exemplars, labels.T)
    return risk, density.reshape(local_q)


def solution(mesh):
    in_specs = (P(("grp", "idx"), None), P("idx", None), P("idx", None))
    out_specs = (P(("grp", "idx"), None), P(("grp", "idx")))
    return jax.shard_map(
        per_device, mesh=mesh, in_specs=in_specs, out_specs=out_specs, check_vma=False
    )
```

```python
import functools
import math

import jax
import jax.numpy as jnp
from jax import lax
from jax.experimental import pallas as pl
from jax.experimental.pallas import tpu as pltpu
from jax.sharding import PartitionSpec as P

X, Z, Y, GROUPS = 4, 8, 2, 4
SHARD = 16
X_ORDER = (0, 1, -1, 2)
Z_ORDER = (0, 1, -1, 2, -2, 3, -3, 4)
PIECES = ((0, 1), (1, 2), (2, 1), (-2, 1), (3, 2), (4, 1))
BLOCK = 256
WIDE = 1024
CATEGORIES = 64
MASS, TOP, DENS, UNUSED = 64, 67, 70, 73
LOG2E = 1.4426950408889634
LOWEST = -1e30
MESH = pl.DeviceIdType.MESH


def lay_out():
    def first(half, *dzs):
        return [(0, dx, dz) for dz in dzs for dx in X_ORDER[2 * half : 2 * half + 2]]

    order = first(0, 0) + first(1, 0) + first(0, 1, -1)
    order += [(1, 0, 0), (1, 0, 1), (1, 0, -1), (1, 0, 2)]
    order += [(1, 1, 0), (1, -1, 0), (1, -1, 1), (1, -1, -1)]
    order += first(1, 1, -1)
    order += [(1, 1, 1), (1, 1, -1), (1, 0, -2), (1, 1, 2), (1, -1, 2), (1, 1, -2), (1, -1, -2)]
    order += [(1, 2, 0), (1, 0, 3), (1, 0, -3), (1, 2, 1), (1, 2, -1)]
    order += first(0, 2, -2) + first(1, 2, -2)
    order += [(1, 0, 4), (1, 2, 2), (1, 2, -2)]
    order += [(1, 1, 3), (1, 1, -3), (1, -1, 3), (1, -1, -3), (1, 1, 4)]
    order += first(0, 3, -3) + first(1, 3, -3) + first(0, 4) + first(1, 4)
    order += [(1, -1, 4), (1, 2, 3), (1, 2, -3), (1, 2, 4)]
    return {place: SHARD * i for i, place in enumerate(order)}


ROW_OF = lay_out()


def row_of(side, dx, dz):
    return ROW_OF[side, dx, dz]


def gather_moves():
    moves = {}
    moves["x2",] = (row_of(0, -1, 0), 1, row_of(0, 2, 0), "xp")
    for half in (0, 1):
        dx = X_ORDER[2 * half]
        for k in (1, 2, 3):
            moves["z+", k, half] = (row_of(0, dx, 1 - k), 2, row_of(0, dx, -k), "zp")
            moves["z-", k, half] = (row_of(0, dx, k - 1), 2, row_of(0, dx, k), "zm")
    moves["z+", 4, 0] = (row_of(0, X_ORDER[0], -2), 2, row_of(0, X_ORDER[0], 4), "zpp")
    moves["z-", 4, 1] = (row_of(0, X_ORDER[2], 2), 2, row_of(0, X_ORDER[2], 4), "zmm")
    for g, (dz, count) in enumerate(PIECES):
        own = row_of(1, 0, dz)
        moves["v+", g] = (own, count, row_of(1, -1, dz), "xp")
        moves["v-", g] = (own, count, row_of(1, 1, dz), "xm")
        if g in (0, 1, 5):
            moves["u+", g] = (row_of(1, -1, dz), count, row_of(1, 2, dz), "xp")
        else:
            moves["u-", g] = (row_of(1, 1, dz), count, row_of(1, 2, dz), "xm")
    moves["w+", 3] = (row_of(1, 0, -2), 1, row_of(1, 0, -3), "zp")
    moves["w-", 3] = (row_of(1, 0, 2), 1, row_of(1, 0, 3), "zm")
    moves["w+", 4] = (row_of(1, 0, -2), 1, row_of(1, 0, 4), "zpp")
    return moves


MOVES = gather_moves()
MOVE_IDS = {name: i for i, name in enumerate(MOVES)}
FIRST_WAY = {(0, dx): len(MOVES) + i for i, dx in enumerate(X_ORDER)}
SECOND_WAY = {dz: len(MOVES) + len(X_ORDER) + i for i, dz in enumerate(Z_ORDER[0:5])}
N_MOVES = len(MOVES) + len(X_ORDER) + 5
SENDERS = X * Z * Y


def dot_t(a, b):
    return lax.dot_general(a, b, (((1,), (1,)), ((), ())), preferred_element_type=jnp.float32)


def kernel(
    groups, total_q, total_e,
    q_ref, ex_hbm, labels_hbm, result_ref,
    rows, ex, labels_raw, labels, s0, s1, s2, s3,
    top_part0, top_part1, row_top, row_sum, peak0, peak1, col_max, col_sum,
    best, hubs, hub_row, numer, arrived,
    load_sem, send, recv, own_send, hub_send, hub_recv, sum_send, sum_recv,
):
    scores = (s0, s1, s2, s3)
    top_part, peak = (top_part0, top_part1), (peak0, peak1)
    depth = q_ref.shape[1]
    gain = 3.0 / math.sqrt(depth) * LOG2E
    local_e = ex.shape[0]
    chunks = local_e // WIDE
    tiles = WIDE // 128
    g = lax.axis_index("grp")
    me = lax.axis_index("idx")
    x, z, y = me // (Z * Y), (me // Y) % Z, me % Y

    def place(dx, dz, y_at):
        return (g, lax.rem(x + dx + X, X) * (Z * Y) + lax.rem(z + dz + Z, Z) * Y + y_at)

    near = {
        "xp": place(1, 0, y), "xm": place(-1, 0, y), "zp": place(0, 1, y), "zm": place(0, -1, y),
        "zpp": place(0, 2, y), "zmm": place(0, -2, y),
    }
    partner = place(0, 0, 1 - y)
    peers = [(lax.rem(g + k, groups), me) for k in range(1, groups)]

    loads = [
        pltpu.make_async_copy(
            ex_hbm.at[pl.ds(n * WIDE, WIDE)], ex.at[pl.ds(n * WIDE, WIDE)], load_sem.at[n]
        )
        for n in range(chunks)
    ]
    label_load = pltpu.make_async_copy(labels_hbm, labels_raw, load_sem.at[chunks])
    label_load.start()
    for load in loads:
        load.start()

    barrier = pltpu.get_barrier_semaphore()
    greeted = [partner, *peers]
    greeted += [place(dx, 0, side) for dx in X_ORDER[1:] for side in (0, 1)]
    greeted += [place(0, dz, side) for dz in Z_ORDER[1:5] for side in (0, 1)]
    for other in greeted:
        pl.semaphore_signal(barrier, inc=1, device_id=other, device_id_type=MESH)
    pl.semaphore_wait(barrier, len(greeted))

    def move(name):
        source, count, target, way = MOVES[name]
        sem = MOVE_IDS[name]
        return pltpu.make_async_remote_copy(
            src_ref=rows.at[pl.ds(source, count * SHARD)],
            dst_ref=rows.at[pl.ds(target, count * SHARD)],
            send_sem=send.at[sem], recv_sem=recv.at[sem],
            device_id=near[way], device_id_type=MESH,
        )

    def go(*names):
        for name in names:
            move(name).start()

    def got(*names):
        for name in names:
            move(name).wait_recv()

    def away(k, target, sem, to):
        return pltpu.make_async_remote_copy(
            src_ref=q_ref, dst_ref=rows.at[pl.ds(target, SHARD)],
            send_sem=own_send.at[k], recv_sem=recv.at[sem], device_id=to, device_id_type=MESH,
        )

    first_away = [away(0, row_of(0, 0, 0), FIRST_WAY[0, 0], partner)]
    for dx in X_ORDER[1:3]:
        for side in (0, 1):
            first_away.append(
                away(len(first_away), row_of(0, -dx, 0), FIRST_WAY[0, -dx], place(dx, 0, side))
            )
    second_away = [away(0, row_of(1, 0, 0), SECOND_WAY[0], partner)]
    for dz in Z_ORDER[1:5]:
        for side in (1, 0):
            second_away.append(
                away(len(second_away), row_of(1, 0, -dz), SECOND_WAY[-dz], place(0, dz, side))
            )

    def landed(target, sem):
        away(0, target, sem, partner).wait_recv()

    own_row = y * row_of(1, 0, 0)
    rows[pl.ds(pl.multiple_of(own_row, SHARD), SHARD), :] = q_ref[...]

    @pl.when(y == 0)
    def _():
        for copy in first_away:
            copy.start()

    @pl.when(y == 1)
    def _():
        for copy in second_away:
            copy.start()
        go(("v+", 0), ("v-", 0))

    label_load.wait()
    rest = lax.broadcasted_iota(jnp.int32, (128 - CATEGORIES, WIDE), 0) + CATEGORIES
    for n in range(chunks):
        at = pl.ds(n * WIDE, WIDE)
        labels[0:CATEGORIES, at] = labels_raw[:, at].astype(jnp.float32).astype(jnp.bfloat16)
        labels[CATEGORIES:128, at] = jnp.where(rest == MASS, 1.0, 0.0).astype(jnp.bfloat16)
    row_sum[...] = jnp.zeros_like(row_sum)
    col_max[...] = jnp.full_like(col_max, LOWEST)
    col_sum[...] = jnp.zeros_like(col_sum)

    @pl.when(y == 0)
    def _():
        landed(row_of(1, 0, 0), SECOND_WAY[0])
        go(("v+", 0), ("v-", 0))

    @pl.when(y == 1)
    def _():
        landed(row_of(0, 0, 0), FIRST_WAY[0, 0])

    landed(row_of(0, 1, 0), FIRST_WAY[0, 1])
    go(("z+", 1, 0), ("z-", 1, 0))
    landed(row_of(0, -1, 0), FIRST_WAY[0, -1])
    go(("x2",))
    landed(row_of(1, 0, 1), SECOND_WAY[1])
    landed(row_of(1, 0, -1), SECOND_WAY[-1])
    go(("v+", 1), ("v-", 1))
    got(("v+", 0), ("v-", 0))
    go(("u+", 0))
    got(("x2",))
    go(("z+", 1, 1), ("z-", 1, 1))
    landed(row_of(1, 0, 2), SECOND_WAY[2])
    go(("w-", 3), ("v+", 2), ("v-", 2))
    landed(row_of(1, 0, -2), SECOND_WAY[-2])
    go(("w+", 3), ("w+", 4), ("v+", 3), ("v-", 3))
    got(("v+", 1))
    go(("u+", 1))
    got(("z+", 1, 0), ("z-", 1, 0))
    go(("z+", 2, 0), ("z-", 2, 0))

    def event(at):
        if at == (0, 3):
            got(("w+", 3), ("w-", 3))
            go(("v+", 4), ("v-", 4))
            got(("v+", 2), ("v-", 2), ("v+", 3), ("v-", 3))
            go(("u-", 2), ("u-", 3))
        if at == (1, 0):
            got(("z+", 1, 1), ("z-", 1, 1))
            go(("z+", 2, 1), ("z-", 2, 1))
            got(("w+", 4))
            go(("v+", 5), ("v-", 5))
            got(("v-", 1), ("u+", 0), ("u+", 1))
        if at == (1, 1):
            got(("z+", 2, 0), ("z-", 2, 0))
            go(("z+", 4, 0), ("z+", 3, 0), ("z-", 3, 0))
        if at == (1, 3):
            got(("v+", 4), ("v-", 4))
            go(("u-", 4))
        if at == (2, 0):
            got(("z+", 2, 1), ("z-", 2, 1))
            go(("z-", 4, 1), ("z+", 3, 1), ("z-", 3, 1))
            got(("v+", 5), ("v-", 5))
            go(("u+", 5))
            got(("u-", 2), ("u-", 3))
        if at == (3, 0):
            got(("z+", 3, 0), ("z-", 3, 0), ("z+", 3, 1), ("z-", 3, 1))
            got(("z+", 4, 0), ("z-", 4, 1), ("u-", 4), ("u+", 5))

    def score(b, n):
        at = pl.ds(n * WIDE, WIDE)
        s = dot_t(rows[pl.ds(b * BLOCK, BLOCK), :], ex[at, :]) * gain
        scores[b][:, at] = s
        top = s[:, 0:128]
        for t in range(1, tiles):
            top = jnp.maximum(top, s[:, t * 128 : (t + 1) * 128])
        ref = top_part[b % 2]
        ref[...] = top if n == 0 else jnp.maximum(ref[...], top)
        peak[b % 2][:, at] = jnp.max(s.reshape(BLOCK // 8, 8, WIDE), axis=0)

    def total(b, n, rowwise=True, colwise=True, tall=32, wide=512):
        at = pl.ds(n * WIDE, WIDE)
        if colwise:
            old = col_max[:, at]
            new = jnp.maximum(old, peak[b % 2][:, at])
            col_max[:, at] = new
            scaled = col_sum[:, at] * jnp.exp2(old - new)
        for c in range(0, WIDE, wide):
            if colwise:
                shift = new[:, c : c + wide]
                col = scaled[:, c : c + wide]
            for r in range(0, BLOCK, tall):
                s = scores[b][r : r + tall, n * WIDE + c : n * WIDE + c + wide]
                if colwise:
                    col = col + jnp.exp2(s.reshape(tall // 8, 8, wide) - shift[None]).sum(0)
                if rowwise:
                    mine = pl.ds(b * BLOCK + r, tall)
                    top = row_top[mine, :]
                    row = row_sum[mine, :]
                    for u in range(0, wide, 128):
                        row = row + jnp.exp2(s[:, u : u + 128] - top)
                    row_sum[mine, :] = row
            if colwise:
                col_sum[:, n * WIDE + c : n * WIDE + c + wide] = col

    def hub_move(k, n):
        at = pl.ds(n * tiles, tiles)
        return pltpu.make_async_remote_copy(
            src_ref=hubs.at[0, at], dst_ref=hubs.at[k, at],
            send_sem=hub_send.at[k, n], recv_sem=hub_recv.at[k, n],
            device_id=peers[k - 1], device_id_type=MESH,
        )

    def hub_part(n):
        at = pl.ds(n * WIDE, WIDE)
        top = jnp.max(col_max[:, at], axis=0, keepdims=True)
        whole = jnp.sum(col_sum[:, at] * jnp.exp2(col_max[:, at] - top), axis=0, keepdims=True)
        lse = top + jnp.log(whole) * LOG2E
        for t in range(tiles):
            hubs[0, n * tiles + t : n * tiles + t + 1, :] = lse[:, t * 128 : (t + 1) * 128]
        for k in range(1, groups):
            hub_move(k, n).start()

    blocks = len(scores)
    final = blocks - 1
    for b in range(blocks):
        for n in range(chunks):
            event((b, n))
            if b == 0:
                loads[n].wait()
            score(b, n)
            if b > 0:
                total(b - 1, n)
            if b == final:
                total(b, n, rowwise=False)
                hub_part(n)
        row_top[pl.ds(b * BLOCK, BLOCK), :] = jnp.broadcast_to(
            jnp.max(top_part[b % 2][...], axis=1, keepdims=True), (BLOCK, 128)
        )
    for n in range(chunks):
        total(final, n, colwise=False)

    for n in range(chunks):
        at = pl.ds(n * tiles, tiles)
        for k in range(1, groups):
            hub_move(k, n).wait_recv()
        parts = [hubs[k, at] for k in range(groups)]
        top = functools.reduce(jnp.maximum, parts)
        whole = sum(jnp.exp2(part - top) for part in parts)
        half_hub = 0.5 * (top + jnp.log(whole) * LOG2E - math.log2(total_q))
        for t in range(tiles):
            hub_row[:, n * WIDE + t * 128 : n * WIDE + (t + 1) * 128] = half_hub[t : t + 1, :]
        for b in range(blocks):
            mine = pl.ds(b * BLOCK, BLOCK)
            top = scores[b][:, n * WIDE : n * WIDE + 128] - hub_row[:, n * WIDE : n * WIDE + 128]
            for t in range(1, tiles):
                at_t = slice(n * WIDE + t * 128, n * WIDE + (t + 1) * 128)
                top = jnp.maximum(top, scores[b][:, at_t] - hub_row[:, at_t])
            best[mine, :] = top if n == 0 else jnp.maximum(best[mine, :], top)

    wide_lane = lax.broadcasted_iota(jnp.int32, (BLOCK, 128), 1)
    half = local_e // 2

    def weigh(b):
        ref = scores[b]
        mine = pl.ds(b * BLOCK, BLOCK)
        top = jnp.max(best[mine, :], axis=1, keepdims=True)
        acc = jnp.zeros((BLOCK, 128), jnp.float32)
        for c in range(0, local_e, half):
            at = slice(c, c + half)
            over = ref[:, at] - hub_row[0:1, at] - top
            weights = jnp.exp2(over + over).astype(jnp.bfloat16)
            acc = acc + dot_t(weights, labels[:, at])
        dens = row_top[mine, :] + LOG2E * jnp.log(
            jnp.sum(row_sum[mine, :], axis=1, keepdims=True)
        )
        figure = jnp.where(
            wide_lane < TOP, acc[:, MASS : MASS + 1], jnp.where(wide_lane < DENS, top, dens)
        )
        high = figure.astype(jnp.bfloat16).astype(jnp.float32)
        middle = (figure - high).astype(jnp.bfloat16).astype(jnp.float32)
        low = figure - high - middle
        turn = lax.rem(wide_lane - MASS, 3)
        piece = jnp.where(turn == 0, high, jnp.where(turn == 1, middle, low))
        piece = jnp.where(wide_lane < UNUSED, piece, 0.0)
        numer[mine, :] = jnp.where(wide_lane < MASS, acc, piece).astype(jnp.bfloat16)

    def slot_of(side, dx, dz):
        return (side * X + X_ORDER.index(dx)) * Z + Z_ORDER.index(dz)

    def sum_move(source, sender, slot, to):
        return pltpu.make_async_remote_copy(
            src_ref=numer.at[pl.ds(source, SHARD)], dst_ref=arrived.at[slot],
            send_sem=sum_send.at[sender], recv_sem=sum_recv.at[slot],
            device_id=to, device_id_type=MESH,
        )

    others = [
        (side, dx, dz)
        for dz in reversed(Z_ORDER)
        for dx in reversed(X_ORDER)
        for side in (0, 1)
        if (dx, dz) != (0, 0)
    ]

    def hand_out(side, dx, dz):
        return sum_move(
            row_of(side, dx, dz), slot_of(side, dx, dz), slot_of(0, dx, dz) + y * (X * Z),
            place(dx, dz, side),
        )

    partner_row = pl.multiple_of((1 - y) * row_of(1, 0, 0), SHARD)
    hand_partner = sum_move(partner_row, 0, y * (X * Z), partner)
    for b in reversed(range(blocks)):
        weigh(b)
        for where in others:
            if row_of(*where) // BLOCK == b:
                hand_out(*where).start()
    hand_partner.start()
    arrived[y * (X * Z)] = numer[pl.ds(pl.multiple_of(own_row, SHARD), SHARD), :]

    for where in others:
        sum_move(0, slot_of(*where), slot_of(*where), partner).wait_recv()
    sum_move(0, 0, (1 - y) * (X * Z), partner).wait_recv()

    parts = arrived[...].astype(jnp.float32)
    lane = lax.broadcasted_iota(jnp.int32, parts.shape, 2)

    def figure_of(first):
        inside = (lane >= first) & (lane < first + 3)
        return jnp.sum(jnp.where(inside, parts, 0.0), axis=2, keepdims=True)

    tops, dens = figure_of(TOP), figure_of(DENS)
    over = tops - jnp.max(tops, axis=0, keepdims=True)
    summed = jnp.sum(parts * jnp.exp2(over + over), axis=0)
    mass = summed[:, MASS : MASS + 1] + summed[:, MASS + 1 : MASS + 2]
    mass = mass + summed[:, MASS + 2 : MASS + 3]
    dens_top = jnp.max(dens, axis=0, keepdims=True)
    dens_sum = jnp.sum(jnp.exp2(dens - dens_top), axis=0)
    density = dens_top[0] / LOG2E + jnp.log(dens_sum) - math.log(total_e)
    result_lane = lax.broadcasted_iota(jnp.int32, (SHARD, 128), 1)
    result_ref[...] = jnp.where(result_lane < CATEGORIES, summed / mass, density)

    @pl.when(y == 0)
    def _():
        for copy in first_away:
            copy.wait_send()

    @pl.when(y == 1)
    def _():
        for copy in second_away:
            copy.wait_send()

    for name in MOVES:
        move(name).wait_send()
    for k in range(1, groups):
        for n in range(chunks):
            hub_move(k, n).wait_send()
    for where in others:
        hand_out(*where).wait_send()
    hand_partner.wait_send()


def split_kernel(result_ref, risk_ref, density_ref):
    risk_ref[...] = result_ref[:, 0:CATEGORIES]
    density_ref[...] = result_ref[...].T[CATEGORIES : CATEGORIES + 1, 0:SHARD]


def per_device(queries, exemplars, labels):
    groups = lax.axis_size("grp")
    devices = lax.axis_size("idx")
    local_q, depth = queries.shape
    local_e = exemplars.shape[0]
    group_q = local_q * devices
    f32, bf16 = jnp.float32, jnp.bfloat16
    vmem, dma = pltpu.VMEM, pltpu.SemaphoreType.DMA
    chunks = local_e // WIDE
    here = pl.BlockSpec(memory_space=pltpu.VMEM)
    away = pl.BlockSpec(memory_space=pl.ANY)
    result = pl.pallas_call(
        functools.partial(kernel, groups, group_q * groups, local_e * devices),
        out_shape=jax.ShapeDtypeStruct((local_q, 128), f32),
        in_specs=[here, away, away],
        out_specs=here,
        scratch_shapes=[
            vmem((group_q, depth), bf16),
            vmem((local_e, depth), bf16),
            vmem((CATEGORIES, local_e), jnp.int32),
            vmem((128, local_e), bf16),
            *[vmem((BLOCK, local_e), f32)] * 4,
            *[vmem((BLOCK, 128), f32)] * 2,
            *[vmem((group_q, 128), f32)] * 2,
            *[vmem((8, local_e), f32)] * 4,
            vmem((group_q, 128), f32),
            vmem((groups, local_e // 128, 128), f32),
            vmem((1, local_e), f32),
            vmem((group_q, 128), bf16),
            vmem((SENDERS, SHARD, 128), bf16),
            dma((chunks + 1,)),
            dma((N_MOVES,)),
            dma((N_MOVES,)),
            dma((9,)),
            dma((groups, chunks)),
            dma((groups, chunks)),
            dma((SENDERS,)),
            dma((SENDERS,)),
        ],
        compiler_params=pltpu.CompilerParams(
            collective_id=0, has_side_effects=True, vmem_limit_bytes=58 * 2**20
        ),
        cost_estimate=pl.CostEstimate(
            flops=2 * group_q * local_e * (depth + 128),
            bytes_accessed=local_e * depth * 2 + local_e * CATEGORIES * 4,
            transcendentals=3 * group_q * local_e,
        ),
        name="prefilter",
    )(queries, exemplars, labels.T)
    risk, density = pl.pallas_call(
        split_kernel,
        out_shape=(
            jax.ShapeDtypeStruct((local_q, CATEGORIES), f32),
            jax.ShapeDtypeStruct((1, local_q), f32),
        ),
        in_specs=[here],
        out_specs=(here, here),
        name="split",
    )(result)
    return risk, density.reshape(local_q)


def solution(mesh):
    in_specs = (P(("grp", "idx"), None), P("idx", None), P("idx", None))
    out_specs = (P(("grp", "idx"), None), P(("grp", "idx")))
    return jax.shard_map(
        per_device, mesh=mesh, in_specs=in_specs, out_specs=out_specs, check_vma=False
    )
```

```python
import functools
import math

import jax
import jax.numpy as jnp
from jax import lax
from jax.experimental import pallas as pl
from jax.experimental.pallas import tpu as pltpu
from jax.sharding import PartitionSpec as P

X, Z, Y, GROUPS = 4, 8, 2, 4
SHARD = 16
X_ORDER = (0, 1, -1, 2)
Z_ORDER = (0, 1, -1, 2, -2, 3, -3, 4)
PIECES = ((0, 1), (1, 2), (2, 1), (-2, 1), (3, 2), (4, 1))
BLOCK = 256
WIDE = 1024
CATEGORIES = 64
MASS, TOP, DENS, UNUSED = 64, 67, 70, 73
LOG2E = 1.4426950408889634
LOWEST = -1e30
MESH = pl.DeviceIdType.MESH


def lay_out():
    def first(half, *dzs):
        return [(0, dx, dz) for dz in dzs for dx in X_ORDER[2 * half : 2 * half + 2]]

    order = first(0, 0) + first(1, 0) + first(0, 1, -1)
    order += [(1, 0, 0), (1, 0, 1), (1, 0, -1), (1, 0, 2)]
    order += [(1, 1, 0), (1, -1, 0), (1, -1, 1), (1, -1, -1)]
    order += first(1, 1, -1)
    order += [(1, 1, 1), (1, 1, -1), (1, 0, -2), (1, 1, 2), (1, -1, 2), (1, 1, -2), (1, -1, -2)]
    order += [(1, 2, 0), (1, 0, 3), (1, 0, -3), (1, 2, 1), (1, 2, -1)]
    order += first(0, 2, -2) + first(1, 2, -2)
    order += [(1, 0, 4), (1, 2, 2), (1, 2, -2)]
    order += [(1, 1, 3), (1, 1, -3), (1, -1, 3), (1, -1, -3), (1, 1, 4)]
    order += first(0, 3, -3) + first(1, 3, -3) + first(0, 4) + first(1, 4)
    order += [(1, -1, 4), (1, 2, 3), (1, 2, -3), (1, 2, 4)]
    return {place: SHARD * i for i, place in enumerate(order)}


ROW_OF = lay_out()


def row_of(side, dx, dz):
    return ROW_OF[side, dx, dz]


def gather_moves():
    moves = {}
    moves["x2",] = (row_of(0, -1, 0), 1, row_of(0, 2, 0), "xp")
    for half in (0, 1):
        dx = X_ORDER[2 * half]
        for k in (1, 2, 3):
            moves["z+", k, half] = (row_of(0, dx, 1 - k), 2, row_of(0, dx, -k), "zp")
            moves["z-", k, half] = (row_of(0, dx, k - 1), 2, row_of(0, dx, k), "zm")
    moves["z+", 4, 0] = (row_of(0, X_ORDER[0], -2), 2, row_of(0, X_ORDER[0], 4), "zpp")
    moves["z-", 4, 1] = (row_of(0, X_ORDER[2], 2), 2, row_of(0, X_ORDER[2], 4), "zmm")
    for g, (dz, count) in enumerate(PIECES):
        own = row_of(1, 0, dz)
        moves["v+", g] = (own, count, row_of(1, -1, dz), "xp")
        moves["v-", g] = (own, count, row_of(1, 1, dz), "xm")
        if g in (0, 1, 5):
            moves["u+", g] = (row_of(1, -1, dz), count, row_of(1, 2, dz), "xp")
        else:
            moves["u-", g] = (row_of(1, 1, dz), count, row_of(1, 2, dz), "xm")
    moves["w+", 3] = (row_of(1, 0, -2), 1, row_of(1, 0, -3), "zp")
    moves["w-", 3] = (row_of(1, 0, 2), 1, row_of(1, 0, 3), "zm")
    moves["w+", 4] = (row_of(1, 0, -2), 1, row_of(1, 0, 4), "zpp")
    return moves


MOVES = gather_moves()
MOVE_IDS = {name: i for i, name in enumerate(MOVES)}
FIRST_WAY = {(0, dx): len(MOVES) + i for i, dx in enumerate(X_ORDER)}
SECOND_WAY = {dz: len(MOVES) + len(X_ORDER) + i for i, dz in enumerate(Z_ORDER[0:5])}
N_MOVES = len(MOVES) + len(X_ORDER) + 5
SENDERS = X * Z * Y


def dot_t(a, b):
    return lax.dot_general(a, b, (((1,), (1,)), ((), ())), preferred_element_type=jnp.float32)


def kernel(
    groups, total_q, total_e,
    q_ref, ex_hbm, labels_hbm, result_ref,
    rows, ex, labels_raw, labels, s0, s1, s2, s3,
    top_part0, top_part1, row_top, row_sum, peak0, peak1, col_max, col_sum,
    best, hubs, hub_row, numer, arrived,
    load_sem, send, recv, own_send, hub_send, hub_recv, sum_send, sum_recv,
):
    scores = (s0, s1, s2, s3)
    top_part, peak = (top_part0, top_part1), (peak0, peak1)
    depth = q_ref.shape[1]
    gain = 3.0 / math.sqrt(depth) * LOG2E
    local_e = ex.shape[0]
    chunks = local_e // WIDE
    tiles = WIDE // 128
    g = lax.axis_index("grp")
    me = lax.axis_index("idx")
    x, z, y = me // (Z * Y), (me // Y) % Z, me % Y

    def place(dx, dz, y_at):
        return (g, lax.rem(x + dx + X, X) * (Z * Y) + lax.rem(z + dz + Z, Z) * Y + y_at)

    near = {
        "xp": place(1, 0, y), "xm": place(-1, 0, y), "zp": place(0, 1, y), "zm": place(0, -1, y),
        "zpp": place(0, 2, y), "zmm": place(0, -2, y),
    }
    partner = place(0, 0, 1 - y)
    peers = [(lax.rem(g + k, groups), me) for k in range(1, groups)]

    loads = [
        pltpu.make_async_copy(
            ex_hbm.at[pl.ds(n * WIDE, WIDE)], ex.at[pl.ds(n * WIDE, WIDE)], load_sem.at[n]
        )
        for n in range(chunks)
    ]
    label_load = pltpu.make_async_copy(labels_hbm, labels_raw, load_sem.at[chunks])
    label_load.start()
    for load in loads:
        load.start()

    barrier = pltpu.get_barrier_semaphore()
    greeted = [partner, *peers]
    greeted += [place(dx, 0, side) for dx in X_ORDER[1:] for side in (0, 1)]
    greeted += [place(0, dz, side) for dz in Z_ORDER[1:5] for side in (0, 1)]
    for other in greeted:
        pl.semaphore_signal(barrier, inc=1, device_id=other, device_id_type=MESH)
    pl.semaphore_wait(barrier, len(greeted))

    def move(name):
        source, count, target, way = MOVES[name]
        sem = MOVE_IDS[name]
        return pltpu.make_async_remote_copy(
            src_ref=rows.at[pl.ds(source, count * SHARD)],
            dst_ref=rows.at[pl.ds(target, count * SHARD)],
            send_sem=send.at[sem], recv_sem=recv.at[sem],
            device_id=near[way], device_id_type=MESH,
        )

    def go(*names):
        for name in names:
            move(name).start()

    def got(*names):
        for name in names:
            move(name).wait_recv()

    def away(k, target, sem, to):
        return pltpu.make_async_remote_copy(
            src_ref=q_ref, dst_ref=rows.at[pl.ds(target, SHARD)],
            send_sem=own_send.at[k], recv_sem=recv.at[sem], device_id=to, device_id_type=MESH,
        )

    first_away = [away(0, row_of(0, 0, 0), FIRST_WAY[0, 0], partner)]
    for dx in X_ORDER[1:3]:
        for side in (0, 1):
            first_away.append(
                away(len(first_away), row_of(0, -dx, 0), FIRST_WAY[0, -dx], place(dx, 0, side))
            )
    second_away = [away(0, row_of(1, 0, 0), SECOND_WAY[0], partner)]
    for dz in Z_ORDER[1:5]:
        for side in (1, 0):
            second_away.append(
                away(len(second_away), row_of(1, 0, -dz), SECOND_WAY[-dz], place(0, dz, side))
            )

    def landed(target, sem):
        away(0, target, sem, partner).wait_recv()

    own_row = y * row_of(1, 0, 0)
    rows[pl.ds(pl.multiple_of(own_row, SHARD), SHARD), :] = q_ref[...]

    @pl.when(y == 0)
    def _():
        for copy in first_away:
            copy.start()

    @pl.when(y == 1)
    def _():
        for copy in second_away:
            copy.start()
        go(("v+", 0), ("v-", 0))

    label_load.wait()
    rest = lax.broadcasted_iota(jnp.int32, (128 - CATEGORIES, WIDE), 0) + CATEGORIES
    for n in range(chunks):
        at = pl.ds(n * WIDE, WIDE)
        labels[0:CATEGORIES, at] = labels_raw[:, at].astype(jnp.float32).astype(jnp.bfloat16)
        labels[CATEGORIES:128, at] = jnp.where(rest == MASS, 1.0, 0.0).astype(jnp.bfloat16)
    row_sum[...] = jnp.zeros_like(row_sum)
    col_max[...] = jnp.full_like(col_max, LOWEST)
    col_sum[...] = jnp.zeros_like(col_sum)

    @pl.when(y == 0)
    def _():
        landed(row_of(1, 0, 0), SECOND_WAY[0])
        go(("v+", 0), ("v-", 0))

    @pl.when(y == 1)
    def _():
        landed(row_of(0, 0, 0), FIRST_WAY[0, 0])

    landed(row_of(0, 1, 0), FIRST_WAY[0, 1])
    go(("z+", 1, 0), ("z-", 1, 0))
    landed(row_of(0, -1, 0), FIRST_WAY[0, -1])
    go(("x2",))
    landed(row_of(1, 0, 1), SECOND_WAY[1])
    landed(row_of(1, 0, -1), SECOND_WAY[-1])
    go(("v+", 1), ("v-", 1))
    got(("v+", 0), ("v-", 0))
    go(("u+", 0))
    got(("x2",))
    go(("z+", 1, 1), ("z-", 1, 1))
    landed(row_of(1, 0, 2), SECOND_WAY[2])
    go(("w-", 3), ("v+", 2), ("v-", 2))
    landed(row_of(1, 0, -2), SECOND_WAY[-2])
    go(("w+", 3), ("w+", 4), ("v+", 3), ("v-", 3))
    got(("v+", 1))
    go(("u+", 1))
    got(("z+", 1, 0), ("z-", 1, 0))
    go(("z+", 2, 0), ("z-", 2, 0))

    def event(at):
        if at == (0, 3):
            got(("w+", 3), ("w-", 3))
            go(("v+", 4), ("v-", 4))
            got(("v+", 2), ("v-", 2), ("v+", 3), ("v-", 3))
            go(("u-", 2), ("u-", 3))
        if at == (1, 0):
            got(("z+", 1, 1), ("z-", 1, 1))
            go(("z+", 2, 1), ("z-", 2, 1))
            got(("w+", 4))
            go(("v+", 5), ("v-", 5))
            got(("v-", 1), ("u+", 0), ("u+", 1))
        if at == (1, 1):
            got(("z+", 2, 0), ("z-", 2, 0))
            go(("z+", 4, 0), ("z+", 3, 0), ("z-", 3, 0))
        if at == (1, 3):
            got(("v+", 4), ("v-", 4))
            go(("u-", 4))
        if at == (2, 0):
            got(("z+", 2, 1), ("z-", 2, 1))
            go(("z-", 4, 1), ("z+", 3, 1), ("z-", 3, 1))
            got(("v+", 5), ("v-", 5))
            go(("u+", 5))
            got(("u-", 2), ("u-", 3))
        if at == (3, 0):
            got(("z+", 3, 0), ("z-", 3, 0), ("z+", 3, 1), ("z-", 3, 1))
            got(("z+", 4, 0), ("z-", 4, 1), ("u-", 4), ("u+", 5))

    def score(b, n):
        at = pl.ds(n * WIDE, WIDE)
        s = dot_t(rows[pl.ds(b * BLOCK, BLOCK), :], ex[at, :]) * gain
        scores[b][:, at] = s
        top = s[:, 0:128]
        for t in range(1, tiles):
            top = jnp.maximum(top, s[:, t * 128 : (t + 1) * 128])
        ref = top_part[b % 2]
        ref[...] = top if n == 0 else jnp.maximum(ref[...], top)
        peak[b % 2][:, at] = jnp.max(s.reshape(BLOCK // 8, 8, WIDE), axis=0)

    def total(b, n, rowwise=True, colwise=True, tall=32, wide=512):
        at = pl.ds(n * WIDE, WIDE)
        if colwise:
            old = col_max[:, at]
            new = jnp.maximum(old, peak[b % 2][:, at])
            col_max[:, at] = new
            scaled = col_sum[:, at] * jnp.exp2(old - new)
        for c in range(0, WIDE, wide):
            if colwise:
                shift = new[:, c : c + wide]
                col = scaled[:, c : c + wide]
            for r in range(0, BLOCK, tall):
                s = scores[b][r : r + tall, n * WIDE + c : n * WIDE + c + wide]
                if colwise:
                    col = col + jnp.exp2(s.reshape(tall // 8, 8, wide) - shift[None]).sum(0)
                if rowwise:
                    mine = pl.ds(b * BLOCK + r, tall)
                    top = row_top[mine, :]
                    row = row_sum[mine, :]
                    for u in range(0, wide, 128):
                        row = row + jnp.exp2(s[:, u : u + 128] - top)
                    row_sum[mine, :] = row
            if colwise:
                col_sum[:, n * WIDE + c : n * WIDE + c + wide] = col

    def hub_move(k, n):
        at = pl.ds(n * tiles, tiles)
        return pltpu.make_async_remote_copy(
            src_ref=hubs.at[0, at], dst_ref=hubs.at[k, at],
            send_sem=hub_send.at[k, n], recv_sem=hub_recv.at[k, n],
            device_id=peers[k - 1], device_id_type=MESH,
        )

    def hub_part(n):
        at = pl.ds(n * WIDE, WIDE)
        top = jnp.max(col_max[:, at], axis=0, keepdims=True)
        whole = jnp.sum(col_sum[:, at] * jnp.exp2(col_max[:, at] - top), axis=0, keepdims=True)
        lse = top + jnp.log(whole) * LOG2E
        for t in range(tiles):
            hubs[0, n * tiles + t : n * tiles + t + 1, :] = lse[:, t * 128 : (t + 1) * 128]
        for k in range(1, groups):
            hub_move(k, n).start()

    blocks = len(scores)
    final = blocks - 1
    for b in range(blocks):
        if b == final:
            for n in range(chunks):
                total(b - 1, n)
        for n in range(chunks):
            event((b, n))
            if b == 0:
                loads[n].wait()
            score(b, n)
            if 0 < b < final:
                total(b - 1, n)
            if b == final:
                total(b, n, rowwise=False)
                hub_part(n)
        row_top[pl.ds(b * BLOCK, BLOCK), :] = jnp.broadcast_to(
            jnp.max(top_part[b % 2][...], axis=1, keepdims=True), (BLOCK, 128)
        )
    for n in range(chunks):
        total(final, n, colwise=False)

    for n in range(chunks):
        at = pl.ds(n * tiles, tiles)
        for k in range(1, groups):
            hub_move(k, n).wait_recv()
        parts = [hubs[k, at] for k in range(groups)]
        top = functools.reduce(jnp.maximum, parts)
        whole = sum(jnp.exp2(part - top) for part in parts)
        half_hub = 0.5 * (top + jnp.log(whole) * LOG2E - math.log2(total_q))
        for t in range(tiles):
            hub_row[:, n * WIDE + t * 128 : n * WIDE + (t + 1) * 128] = half_hub[t : t + 1, :]
        for b in range(blocks):
            mine = pl.ds(b * BLOCK, BLOCK)
            top = scores[b][:, n * WIDE : n * WIDE + 128] - hub_row[:, n * WIDE : n * WIDE + 128]
            for t in range(1, tiles):
                at_t = slice(n * WIDE + t * 128, n * WIDE + (t + 1) * 128)
                top = jnp.maximum(top, scores[b][:, at_t] - hub_row[:, at_t])
            best[mine, :] = top if n == 0 else jnp.maximum(best[mine, :], top)

    wide_lane = lax.broadcasted_iota(jnp.int32, (BLOCK, 128), 1)
    half = local_e // 2

    def weigh(b):
        ref = scores[b]
        mine = pl.ds(b * BLOCK, BLOCK)
        top = jnp.max(best[mine, :], axis=1, keepdims=True)
        acc = jnp.zeros((BLOCK, 128), jnp.float32)
        for c in range(0, local_e, half):
            at = slice(c, c + half)
            over = ref[:, at] - hub_row[0:1, at] - top
            weights = jnp.exp2(over + over).astype(jnp.bfloat16)
            acc = acc + dot_t(weights, labels[:, at])
        dens = row_top[mine, :] + LOG2E * jnp.log(
            jnp.sum(row_sum[mine, :], axis=1, keepdims=True)
        )
        figure = jnp.where(
            wide_lane < TOP, acc[:, MASS : MASS + 1], jnp.where(wide_lane < DENS, top, dens)
        )
        high = figure.astype(jnp.bfloat16).astype(jnp.float32)
        middle = (figure - high).astype(jnp.bfloat16).astype(jnp.float32)
        low = figure - high - middle
        turn = lax.rem(wide_lane - MASS, 3)
        piece = jnp.where(turn == 0, high, jnp.where(turn == 1, middle, low))
        piece = jnp.where(wide_lane < UNUSED, piece, 0.0)
        numer[mine, :] = jnp.where(wide_lane < MASS, acc, piece).astype(jnp.bfloat16)

    def slot_of(side, dx, dz):
        return (side * X + X_ORDER.index(dx)) * Z + Z_ORDER.index(dz)

    def sum_move(source, sender, slot, to):
        return pltpu.make_async_remote_copy(
            src_ref=numer.at[pl.ds(source, SHARD)], dst_ref=arrived.at[slot],
            send_sem=sum_send.at[sender], recv_sem=sum_recv.at[slot],
            device_id=to, device_id_type=MESH,
        )

    others = [
        (side, dx, dz)
        for dz in reversed(Z_ORDER)
        for dx in reversed(X_ORDER)
        for side in (0, 1)
        if (dx, dz) != (0, 0)
    ]

    def hand_out(side, dx, dz):
        return sum_move(
            row_of(side, dx, dz), slot_of(side, dx, dz), slot_of(0, dx, dz) + y * (X * Z),
            place(dx, dz, side),
        )

    partner_row = pl.multiple_of((1 - y) * row_of(1, 0, 0), SHARD)
    hand_partner = sum_move(partner_row, 0, y * (X * Z), partner)
    for b in reversed(range(blocks)):
        weigh(b)
        for where in others:
            if row_of(*where) // BLOCK == b:
                hand_out(*where).start()
    hand_partner.start()
    arrived[y * (X * Z)] = numer[pl.ds(pl.multiple_of(own_row, SHARD), SHARD), :]

    lane = lax.broadcasted_iota(jnp.int32, (SHARD, 128), 1)
    in_top = (lane >= TOP) & (lane < DENS)
    in_dens = (lane >= DENS) & (lane < UNUSED)

    def join(slots):
        parts = [arrived[slot].astype(jnp.float32) for slot in slots]
        tops = [jnp.sum(jnp.where(in_top, p, 0.0), axis=1, keepdims=True) for p in parts]
        dens = [jnp.sum(jnp.where(in_dens, p, 0.0), axis=1, keepdims=True) for p in parts]
        top = functools.reduce(jnp.maximum, tops)
        dens_top = functools.reduce(jnp.maximum, dens)
        summed = jnp.zeros((SHARD, 128), jnp.float32)
        dens_sum = jnp.zeros((SHARD, 1), jnp.float32)
        for part, mine, own_dens in zip(parts, tops, dens):
            summed = summed + part * jnp.exp2(2.0 * (mine - top))
            dens_sum = dens_sum + jnp.exp2(own_dens - dens_top)
        return top, summed, dens_top, dens_sum

    late = {
        (dx, dz)
        for side, dx, dz in ROW_OF
        if row_of(side, dx, dz) < BLOCK
    }
    early_slots = [slot_of(*where) for where in others if where[1:] not in late]
    late_slots = [slot_of(*where) for where in others if where[1:] in late]
    for slot in early_slots:
        sum_move(0, slot, slot, partner).wait_recv()
    top_a, summed_a, dens_top_a, dens_sum_a = join(early_slots)
    for slot in late_slots:
        sum_move(0, slot, slot, partner).wait_recv()
    sum_move(0, 0, (1 - y) * (X * Z), partner).wait_recv()
    top_b, summed_b, dens_top_b, dens_sum_b = join([*late_slots, 0, X * Z])
    top = jnp.maximum(top_a, top_b)
    summed = summed_a * jnp.exp2(2.0 * (top_a - top)) + summed_b * jnp.exp2(2.0 * (top_b - top))
    mass = summed[:, MASS : MASS + 1] + summed[:, MASS + 1 : MASS + 2]
    mass = mass + summed[:, MASS + 2 : MASS + 3]
    dens_top = jnp.maximum(dens_top_a, dens_top_b)
    dens_sum = dens_sum_a * jnp.exp2(dens_top_a - dens_top)
    dens_sum = dens_sum + dens_sum_b * jnp.exp2(dens_top_b - dens_top)
    density = dens_top / LOG2E + jnp.log(dens_sum) - math.log(total_e)
    result_lane = lax.broadcasted_iota(jnp.int32, (SHARD, 128), 1)
    result_ref[...] = jnp.where(result_lane < CATEGORIES, summed / mass, density)

    @pl.when(y == 0)
    def _():
        for copy in first_away:
            copy.wait_send()

    @pl.when(y == 1)
    def _():
        for copy in second_away:
            copy.wait_send()

    for name in MOVES:
        move(name).wait_send()
    for k in range(1, groups):
        for n in range(chunks):
            hub_move(k, n).wait_send()
    for where in others:
        hand_out(*where).wait_send()
    hand_partner.wait_send()


def split_kernel(result_ref, risk_ref, density_ref):
    risk_ref[...] = result_ref[:, 0:CATEGORIES]
    density_ref[...] = result_ref[...].T[CATEGORIES : CATEGORIES + 1, 0:SHARD]


def per_device(queries, exemplars, labels):
    groups = lax.axis_size("grp")
    devices = lax.axis_size("idx")
    local_q, depth = queries.shape
    local_e = exemplars.shape[0]
    group_q = local_q * devices
    f32, bf16 = jnp.float32, jnp.bfloat16
    vmem, dma = pltpu.VMEM, pltpu.SemaphoreType.DMA
    chunks = local_e // WIDE
    here = pl.BlockSpec(memory_space=pltpu.VMEM)
    away = pl.BlockSpec(memory_space=pl.ANY)
    result = pl.pallas_call(
        functools.partial(kernel, groups, group_q * groups, local_e * devices),
        out_shape=jax.ShapeDtypeStruct((local_q, 128), f32),
        in_specs=[here, away, away],
        out_specs=here,
        scratch_shapes=[
            vmem((group_q, depth), bf16),
            vmem((local_e, depth), bf16),
            vmem((CATEGORIES, local_e), jnp.int32),
            vmem((128, local_e), bf16),
            *[vmem((BLOCK, local_e), f32)] * 4,
            *[vmem((BLOCK, 128), f32)] * 2,
            *[vmem((group_q, 128), f32)] * 2,
            *[vmem((8, local_e), f32)] * 4,
            vmem((group_q, 128), f32),
            vmem((groups, local_e // 128, 128), f32),
            vmem((1, local_e), f32),
            vmem((group_q, 128), bf16),
            vmem((SENDERS, SHARD, 128), bf16),
            dma((chunks + 1,)),
            dma((N_MOVES,)),
            dma((N_MOVES,)),
            dma((9,)),
            dma((groups, chunks)),
            dma((groups, chunks)),
            dma((SENDERS,)),
            dma((SENDERS,)),
        ],
        compiler_params=pltpu.CompilerParams(
            collective_id=0, has_side_effects=True, vmem_limit_bytes=58 * 2**20
        ),
        cost_estimate=pl.CostEstimate(
            flops=2 * group_q * local_e * (depth + 128),
            bytes_accessed=local_e * depth * 2 + local_e * CATEGORIES * 4,
            transcendentals=3 * group_q * local_e,
        ),
        name="prefilter",
    )(queries, exemplars, labels.T)
    risk, density = pl.pallas_call(
        split_kernel,
        out_shape=(
            jax.ShapeDtypeStruct((local_q, CATEGORIES), f32),
            jax.ShapeDtypeStruct((1, local_q), f32),
        ),
        in_specs=[here],
        out_specs=(here, here),
        name="split",
    )(result)
    return risk, density.reshape(local_q)


def solution(mesh):
    in_specs = (P(("grp", "idx"), None), P("idx", None), P("idx", None))
    out_specs = (P(("grp", "idx"), None), P(("grp", "idx")))
    return jax.shard_map(
        per_device, mesh=mesh, in_specs=in_specs, out_specs=out_specs, check_vma=False
    )
```

```python
import functools
import math

import jax
import jax.numpy as jnp
from jax import lax
from jax.experimental import pallas as pl
from jax.experimental.pallas import tpu as pltpu
from jax.sharding import PartitionSpec as P

X, Z, Y, GROUPS = 4, 8, 2, 4
SHARD = 16
X_ORDER = (0, 1, -1, 2)
Z_ORDER = (0, 1, -1, 2, -2, 3, -3, 4)
PIECES = ((0, 1), (1, 2), (2, 1), (-2, 1), (3, 2), (4, 1))
BLOCK = 256
WIDE = 1024
CATEGORIES = 64
MASS, TOP, DENS, UNUSED = 64, 67, 70, 73
LOG2E = 1.4426950408889634
LOWEST = -1e30
MESH = pl.DeviceIdType.MESH


def lay_out():
    def first(half, *dzs):
        return [(0, dx, dz) for dz in dzs for dx in X_ORDER[2 * half : 2 * half + 2]]

    order = first(0, 0) + first(1, 0) + first(0, 1, -1)
    order += [(1, 0, 0), (1, 0, 1), (1, 0, -1), (1, 0, 2)]
    order += [(1, 1, 0), (1, -1, 0), (1, -1, 1), (1, -1, -1)]
    order += first(1, 1, -1)
    order += [(1, 1, 1), (1, 1, -1), (1, 0, -2), (1, 1, 2), (1, -1, 2), (1, 1, -2), (1, -1, -2)]
    order += [(1, 2, 0), (1, 0, 3), (1, 0, -3), (1, 2, 1), (1, 2, -1)]
    order += first(0, 2, -2) + first(1, 2, -2)
    order += [(1, 0, 4), (1, 2, 2), (1, 2, -2)]
    order += [(1, 1, 3), (1, 1, -3), (1, -1, 3), (1, -1, -3), (1, 1, 4)]
    order += first(0, 3, -3) + first(1, 3, -3) + first(0, 4) + first(1, 4)
    order += [(1, -1, 4), (1, 2, 3), (1, 2, -3), (1, 2, 4)]
    return {place: SHARD * i for i, place in enumerate(order)}


ROW_OF = lay_out()


def row_of(side, dx, dz):
    return ROW_OF[side, dx, dz]


def gather_moves():
    moves = {}
    moves["x2",] = (row_of(0, -1, 0), 1, row_of(0, 2, 0), "xp")
    for half in (0, 1):
        dx = X_ORDER[2 * half]
        for k in (1, 2, 3):
            moves["z+", k, half] = (row_of(0, dx, 1 - k), 2, row_of(0, dx, -k), "zp")
            moves["z-", k, half] = (row_of(0, dx, k - 1), 2, row_of(0, dx, k), "zm")
    moves["z+", 4, 0] = (row_of(0, X_ORDER[0], -2), 2, row_of(0, X_ORDER[0], 4), "zpp")
    moves["z-", 4, 1] = (row_of(0, X_ORDER[2], 2), 2, row_of(0, X_ORDER[2], 4), "zmm")
    for g, (dz, count) in enumerate(PIECES):
        own = row_of(1, 0, dz)
        moves["v+", g] = (own, count, row_of(1, -1, dz), "xp")
        moves["v-", g] = (own, count, row_of(1, 1, dz), "xm")
        if g in (0, 1, 5):
            moves["u+", g] = (row_of(1, -1, dz), count, row_of(1, 2, dz), "xp")
        else:
            moves["u-", g] = (row_of(1, 1, dz), count, row_of(1, 2, dz), "xm")
    moves["w+", 3] = (row_of(1, 0, -2), 1, row_of(1, 0, -3), "zp")
    moves["w-", 3] = (row_of(1, 0, 2), 1, row_of(1, 0, 3), "zm")
    moves["w+", 4] = (row_of(1, 0, -2), 1, row_of(1, 0, 4), "zpp")
    return moves


MOVES = gather_moves()
MOVE_IDS = {name: i for i, name in enumerate(MOVES)}
FIRST_WAY = {(0, dx): len(MOVES) + i for i, dx in enumerate(X_ORDER)}
SECOND_WAY = {dz: len(MOVES) + len(X_ORDER) + i for i, dz in enumerate(Z_ORDER[0:5])}
N_MOVES = len(MOVES) + len(X_ORDER) + 5
SENDERS = X * Z * Y


def dot_t(a, b):
    return lax.dot_general(a, b, (((1,), (1,)), ((), ())), preferred_element_type=jnp.float32)


def kernel(
    groups, total_q, total_e,
    q_ref, ex_hbm, labels_hbm, result_ref,
    rows, ex, labels_raw, labels, s0, s1, s2, s3,
    top_part0, top_part1, row_top, row_sum, peak0, peak1, col_max, col_sum,
    best, hubs, hub_row, numer, arrived,
    load_sem, send, recv, own_send, hub_send, hub_recv, sum_send, sum_recv,
):
    scores = (s0, s1, s2, s3)
    top_part, peak = (top_part0, top_part1), (peak0, peak1)
    depth = q_ref.shape[1]
    gain = 3.0 / math.sqrt(depth) * LOG2E
    local_e = ex.shape[0]
    chunks = local_e // WIDE
    tiles = WIDE // 128
    g = lax.axis_index("grp")
    me = lax.axis_index("idx")
    x, z, y = me // (Z * Y), (me // Y) % Z, me % Y

    def place(dx, dz, y_at):
        return (g, lax.rem(x + dx + X, X) * (Z * Y) + lax.rem(z + dz + Z, Z) * Y + y_at)

    near = {
        "xp": place(1, 0, y), "xm": place(-1, 0, y), "zp": place(0, 1, y), "zm": place(0, -1, y),
        "zpp": place(0, 2, y), "zmm": place(0, -2, y),
    }
    partner = place(0, 0, 1 - y)
    peers = [(lax.rem(g + k, groups), me) for k in range(1, groups)]

    loads = [
        pltpu.make_async_copy(
            ex_hbm.at[pl.ds(n * WIDE, WIDE)], ex.at[pl.ds(n * WIDE, WIDE)], load_sem.at[n]
        )
        for n in range(chunks)
    ]
    label_load = pltpu.make_async_copy(labels_hbm, labels_raw, load_sem.at[chunks])
    label_load.start()
    for load in loads:
        load.start()

    barrier = pltpu.get_barrier_semaphore()
    greeted = [partner, *peers]
    greeted += [place(dx, 0, side) for dx in X_ORDER[1:3] for side in (0, 1)]
    greeted += [place(0, dz, side) for dz in Z_ORDER[1:5] for side in (0, 1)]
    for other in greeted:
        pl.semaphore_signal(barrier, inc=1, device_id=other, device_id_type=MESH)
    pl.semaphore_wait(barrier, len(greeted))

    def move(name):
        source, count, target, way = MOVES[name]
        sem = MOVE_IDS[name]
        return pltpu.make_async_remote_copy(
            src_ref=rows.at[pl.ds(source, count * SHARD)],
            dst_ref=rows.at[pl.ds(target, count * SHARD)],
            send_sem=send.at[sem], recv_sem=recv.at[sem],
            device_id=near[way], device_id_type=MESH,
        )

    def go(*names):
        for name in names:
            move(name).start()

    def got(*names):
        for name in names:
            move(name).wait_recv()

    def away(k, target, sem, to):
        return pltpu.make_async_remote_copy(
            src_ref=q_ref, dst_ref=rows.at[pl.ds(target, SHARD)],
            send_sem=own_send.at[k], recv_sem=recv.at[sem], device_id=to, device_id_type=MESH,
        )

    first_away = [away(0, row_of(0, 0, 0), FIRST_WAY[0, 0], partner)]
    for dx in X_ORDER[1:3]:
        for side in (0, 1):
            first_away.append(
                away(len(first_away), row_of(0, -dx, 0), FIRST_WAY[0, -dx], place(dx, 0, side))
            )
    second_away = [away(0, row_of(1, 0, 0), SECOND_WAY[0], partner)]
    for dz in Z_ORDER[1:5]:
        for side in (1, 0):
            second_away.append(
                away(len(second_away), row_of(1, 0, -dz), SECOND_WAY[-dz], place(0, dz, side))
            )

    def landed(target, sem):
        away(0, target, sem, partner).wait_recv()

    own_row = y * row_of(1, 0, 0)
    rows[pl.ds(pl.multiple_of(own_row, SHARD), SHARD), :] = q_ref[...]

    @pl.when(y == 0)
    def _():
        for copy in first_away:
            copy.start()

    @pl.when(y == 1)
    def _():
        for copy in second_away:
            copy.start()
        go(("v+", 0), ("v-", 0))

    label_load.wait()
    rest = lax.broadcasted_iota(jnp.int32, (128 - CATEGORIES, WIDE), 0) + CATEGORIES
    for n in range(chunks):
        at = pl.ds(n * WIDE, WIDE)
        labels[0:CATEGORIES, at] = labels_raw[:, at].astype(jnp.float32).astype(jnp.bfloat16)
        labels[CATEGORIES:128, at] = jnp.where(rest == MASS, 1.0, 0.0).astype(jnp.bfloat16)
    row_sum[...] = jnp.zeros_like(row_sum)
    col_max[...] = jnp.full_like(col_max, LOWEST)
    col_sum[...] = jnp.zeros_like(col_sum)

    @pl.when(y == 0)
    def _():
        landed(row_of(1, 0, 0), SECOND_WAY[0])
        go(("v+", 0), ("v-", 0))

    @pl.when(y == 1)
    def _():
        landed(row_of(0, 0, 0), FIRST_WAY[0, 0])

    landed(row_of(0, 1, 0), FIRST_WAY[0, 1])
    go(("z+", 1, 0), ("z-", 1, 0))
    landed(row_of(0, -1, 0), FIRST_WAY[0, -1])
    go(("x2",))
    landed(row_of(1, 0, 1), SECOND_WAY[1])
    landed(row_of(1, 0, -1), SECOND_WAY[-1])
    go(("v+", 1), ("v-", 1))
    got(("v+", 0), ("v-", 0))
    go(("u+", 0))
    got(("x2",))
    go(("z+", 1, 1), ("z-", 1, 1))
    landed(row_of(1, 0, 2), SECOND_WAY[2])
    go(("w-", 3), ("v+", 2), ("v-", 2))
    landed(row_of(1, 0, -2), SECOND_WAY[-2])
    go(("w+", 3), ("w+", 4), ("v+", 3), ("v-", 3))
    got(("v+", 1))
    go(("u+", 1))
    got(("z+", 1, 0), ("z-", 1, 0))
    go(("z+", 2, 0), ("z-", 2, 0))

    def event(at):
        if at == (0, 3):
            got(("w+", 3), ("w-", 3))
            go(("v+", 4), ("v-", 4))
            got(("v+", 2), ("v-", 2), ("v+", 3), ("v-", 3))
            go(("u-", 2), ("u-", 3))
        if at == (1, 0):
            got(("z+", 1, 1), ("z-", 1, 1))
            go(("z+", 2, 1), ("z-", 2, 1))
            got(("w+", 4))
            go(("v+", 5), ("v-", 5))
            got(("v-", 1), ("u+", 0), ("u+", 1))
        if at == (1, 1):
            got(("z+", 2, 0), ("z-", 2, 0))
            go(("z+", 4, 0), ("z+", 3, 0), ("z-", 3, 0))
        if at == (1, 3):
            got(("v+", 4), ("v-", 4))
            go(("u-", 4))
        if at == (2, 0):
            got(("z+", 2, 1), ("z-", 2, 1))
            go(("z-", 4, 1), ("z+", 3, 1), ("z-", 3, 1))
            got(("v+", 5), ("v-", 5))
            go(("u+", 5))
            got(("u-", 2), ("u-", 3))
        if at == (3, 0):
            got(("z+", 3, 0), ("z-", 3, 0), ("z+", 3, 1), ("z-", 3, 1))
            got(("z+", 4, 0), ("z-", 4, 1), ("u-", 4), ("u+", 5))

    def score(b, n):
        at = pl.ds(n * WIDE, WIDE)
        s = dot_t(rows[pl.ds(b * BLOCK, BLOCK), :], ex[at, :]) * gain
        scores[b][:, at] = s
        top = s[:, 0:128]
        for t in range(1, tiles):
            top = jnp.maximum(top, s[:, t * 128 : (t + 1) * 128])
        ref = top_part[b % 2]
        ref[...] = top if n == 0 else jnp.maximum(ref[...], top)
        peak[b % 2][:, at] = jnp.max(s.reshape(BLOCK // 8, 8, WIDE), axis=0)

    def total(b, n, rowwise=True, colwise=True, tall=32, wide=512):
        at = pl.ds(n * WIDE, WIDE)
        if colwise:
            old = col_max[:, at]
            new = jnp.maximum(old, peak[b % 2][:, at])
            col_max[:, at] = new
            scaled = col_sum[:, at] * jnp.exp2(old - new)
        for c in range(0, WIDE, wide):
            if colwise:
                shift = new[:, c : c + wide]
                col = scaled[:, c : c + wide]
            for r in range(0, BLOCK, tall):
                s = scores[b][r : r + tall, n * WIDE + c : n * WIDE + c + wide]
                if colwise:
                    col = col + jnp.exp2(s.reshape(tall // 8, 8, wide) - shift[None]).sum(0)
                if rowwise:
                    mine = pl.ds(b * BLOCK + r, tall)
                    top = row_top[mine, :]
                    row = row_sum[mine, :]
                    for u in range(0, wide, 128):
                        row = row + jnp.exp2(s[:, u : u + 128] - top)
                    row_sum[mine, :] = row
            if colwise:
                col_sum[:, n * WIDE + c : n * WIDE + c + wide] = col

    def hub_move(k, n):
        at = pl.ds(n * tiles, tiles)
        return pltpu.make_async_remote_copy(
            src_ref=hubs.at[0, at], dst_ref=hubs.at[k, at],
            send_sem=hub_send.at[k, n], recv_sem=hub_recv.at[k, n],
            device_id=peers[k - 1], device_id_type=MESH,
        )

    def hub_part(n):
        at = pl.ds(n * WIDE, WIDE)
        top = jnp.max(col_max[:, at], axis=0, keepdims=True)
        whole = jnp.sum(col_sum[:, at] * jnp.exp2(col_max[:, at] - top), axis=0, keepdims=True)
        lse = top + jnp.log(whole) * LOG2E
        for t in range(tiles):
            hubs[0, n * tiles + t : n * tiles + t + 1, :] = lse[:, t * 128 : (t + 1) * 128]
        for k in range(1, groups):
            hub_move(k, n).start()

    blocks = len(scores)
    final = blocks - 1
    for b in range(blocks):
        if b == final:
            for n in range(chunks):
                total(b - 1, n)
        for n in range(chunks):
            event((b, n))
            if b == 0:
                loads[n].wait()
            score(b, n)
            if 0 < b < final:
                total(b - 1, n)
            if b == final:
                total(b, n, rowwise=False)
                hub_part(n)
        row_top[pl.ds(b * BLOCK, BLOCK), :] = jnp.broadcast_to(
            jnp.max(top_part[b % 2][...], axis=1, keepdims=True), (BLOCK, 128)
        )
    for n in range(chunks):
        total(final, n, colwise=False)

    for n in range(chunks):
        at = pl.ds(n * tiles, tiles)
        for k in range(1, groups):
            hub_move(k, n).wait_recv()
        parts = [hubs[k, at] for k in range(groups)]
        top = functools.reduce(jnp.maximum, parts)
        whole = sum(jnp.exp2(part - top) for part in parts)
        half_hub = 0.5 * (top + jnp.log(whole) * LOG2E - math.log2(total_q))
        for t in range(tiles):
            hub_row[:, n * WIDE + t * 128 : n * WIDE + (t + 1) * 128] = half_hub[t : t + 1, :]
        for b in range(blocks):
            mine = pl.ds(b * BLOCK, BLOCK)
            top = scores[b][:, n * WIDE : n * WIDE + 128] - hub_row[:, n * WIDE : n * WIDE + 128]
            for t in range(1, tiles):
                at_t = slice(n * WIDE + t * 128, n * WIDE + (t + 1) * 128)
                top = jnp.maximum(top, scores[b][:, at_t] - hub_row[:, at_t])
            best[mine, :] = top if n == 0 else jnp.maximum(best[mine, :], top)

    wide_lane = lax.broadcasted_iota(jnp.int32, (BLOCK, 128), 1)
    half = local_e // 2

    def weigh(b):
        ref = scores[b]
        mine = pl.ds(b * BLOCK, BLOCK)
        top = jnp.max(best[mine, :], axis=1, keepdims=True)
        acc = jnp.zeros((BLOCK, 128), jnp.float32)
        for c in range(0, local_e, half):
            at = slice(c, c + half)
            over = ref[:, at] - hub_row[0:1, at] - top
            weights = jnp.exp2(over + over).astype(jnp.bfloat16)
            acc = acc + dot_t(weights, labels[:, at])
        dens = row_top[mine, :] + LOG2E * jnp.log(
            jnp.sum(row_sum[mine, :], axis=1, keepdims=True)
        )
        figure = jnp.where(
            wide_lane < TOP, acc[:, MASS : MASS + 1], jnp.where(wide_lane < DENS, top, dens)
        )
        high = figure.astype(jnp.bfloat16).astype(jnp.float32)
        middle = (figure - high).astype(jnp.bfloat16).astype(jnp.float32)
        low = figure - high - middle
        turn = lax.rem(wide_lane - MASS, 3)
        piece = jnp.where(turn == 0, high, jnp.where(turn == 1, middle, low))
        piece = jnp.where(wide_lane < UNUSED, piece, 0.0)
        numer[mine, :] = jnp.where(wide_lane < MASS, acc, piece).astype(jnp.bfloat16)

    def slot_of(side, dx, dz):
        return (side * X + X_ORDER.index(dx)) * Z + Z_ORDER.index(dz)

    def sum_move(source, sender, slot, to):
        return pltpu.make_async_remote_copy(
            src_ref=numer.at[pl.ds(source, SHARD)], dst_ref=arrived.at[slot],
            send_sem=sum_send.at[sender], recv_sem=sum_recv.at[slot],
            device_id=to, device_id_type=MESH,
        )

    others = [
        (side, dx, dz)
        for dz in reversed(Z_ORDER)
        for dx in reversed(X_ORDER)
        for side in (0, 1)
        if (dx, dz) != (0, 0)
    ]

    def hand_out(side, dx, dz):
        return sum_move(
            row_of(side, dx, dz), slot_of(side, dx, dz), slot_of(0, dx, dz) + y * (X * Z),
            place(dx, dz, side),
        )

    partner_row = pl.multiple_of((1 - y) * row_of(1, 0, 0), SHARD)
    hand_partner = sum_move(partner_row, 0, y * (X * Z), partner)
    for b in reversed(range(blocks)):
        weigh(b)
        for where in others:
            if row_of(*where) // BLOCK == b:
                hand_out(*where).start()
    hand_partner.start()
    arrived[y * (X * Z)] = numer[pl.ds(pl.multiple_of(own_row, SHARD), SHARD), :]

    lane = lax.broadcasted_iota(jnp.int32, (SHARD, 128), 1)
    in_top = (lane >= TOP) & (lane < DENS)
    in_dens = (lane >= DENS) & (lane < UNUSED)

    def join(slots):
        parts = [arrived[slot].astype(jnp.float32) for slot in slots]
        tops = [jnp.sum(jnp.where(in_top, p, 0.0), axis=1, keepdims=True) for p in parts]
        dens = [jnp.sum(jnp.where(in_dens, p, 0.0), axis=1, keepdims=True) for p in parts]
        top = functools.reduce(jnp.maximum, tops)
        dens_top = functools.reduce(jnp.maximum, dens)
        summed = jnp.zeros((SHARD, 128), jnp.float32)
        dens_sum = jnp.zeros((SHARD, 1), jnp.float32)
        for part, mine, own_dens in zip(parts, tops, dens):
            summed = summed + part * jnp.exp2(2.0 * (mine - top))
            dens_sum = dens_sum + jnp.exp2(own_dens - dens_top)
        return top, summed, dens_top, dens_sum

    late = {
        (dx, dz)
        for side, dx, dz in ROW_OF
        if row_of(side, dx, dz) < BLOCK
    }
    early_slots = [slot_of(*where) for where in others if where[1:] not in late]
    late_slots = [slot_of(*where) for where in others if where[1:] in late]
    for slot in early_slots:
        sum_move(0, slot, slot, partner).wait_recv()
    top_a, summed_a, dens_top_a, dens_sum_a = join(early_slots)
    for slot in late_slots:
        sum_move(0, slot, slot, partner).wait_recv()
    sum_move(0, 0, (1 - y) * (X * Z), partner).wait_recv()
    top_b, summed_b, dens_top_b, dens_sum_b = join([*late_slots, 0, X * Z])
    top = jnp.maximum(top_a, top_b)
    summed = summed_a * jnp.exp2(2.0 * (top_a - top)) + summed_b * jnp.exp2(2.0 * (top_b - top))
    mass = summed[:, MASS : MASS + 1] + summed[:, MASS + 1 : MASS + 2]
    mass = mass + summed[:, MASS + 2 : MASS + 3]
    dens_top = jnp.maximum(dens_top_a, dens_top_b)
    dens_sum = dens_sum_a * jnp.exp2(dens_top_a - dens_top)
    dens_sum = dens_sum + dens_sum_b * jnp.exp2(dens_top_b - dens_top)
    density = dens_top / LOG2E + jnp.log(dens_sum) - math.log(total_e)
    result_lane = lax.broadcasted_iota(jnp.int32, (SHARD, 128), 1)
    result_ref[...] = jnp.where(result_lane < CATEGORIES, summed / mass, density)

    @pl.when(y == 0)
    def _():
        for copy in first_away:
            copy.wait_send()

    @pl.when(y == 1)
    def _():
        for copy in second_away:
            copy.wait_send()

    for name in MOVES:
        move(name).wait_send()
    for k in range(1, groups):
        for n in range(chunks):
            hub_move(k, n).wait_send()
    for where in others:
        hand_out(*where).wait_send()
    hand_partner.wait_send()


def split_kernel(result_ref, risk_ref, density_ref):
    risk_ref[...] = result_ref[:, 0:CATEGORIES]
    density_ref[...] = result_ref[...].T[CATEGORIES : CATEGORIES + 1, 0:SHARD]


def per_device(queries, exemplars, labels):
    groups = lax.axis_size("grp")
    devices = lax.axis_size("idx")
    local_q, depth = queries.shape
    local_e = exemplars.shape[0]
    group_q = local_q * devices
    f32, bf16 = jnp.float32, jnp.bfloat16
    vmem, dma = pltpu.VMEM, pltpu.SemaphoreType.DMA
    chunks = local_e // WIDE
    here = pl.BlockSpec(memory_space=pltpu.VMEM)
    away = pl.BlockSpec(memory_space=pl.ANY)
    result = pl.pallas_call(
        functools.partial(kernel, groups, group_q * groups, local_e * devices),
        out_shape=jax.ShapeDtypeStruct((local_q, 128), f32),
        in_specs=[here, away, away],
        out_specs=here,
        scratch_shapes=[
            vmem((group_q, depth), bf16),
            vmem((local_e, depth), bf16),
            vmem((CATEGORIES, local_e), jnp.int32),
            vmem((128, local_e), bf16),
            *[vmem((BLOCK, local_e), f32)] * 4,
            *[vmem((BLOCK, 128), f32)] * 2,
            *[vmem((group_q, 128), f32)] * 2,
            *[vmem((8, local_e), f32)] * 4,
            vmem((group_q, 128), f32),
            vmem((groups, local_e // 128, 128), f32),
            vmem((1, local_e), f32),
            vmem((group_q, 128), bf16),
            vmem((SENDERS, SHARD, 128), bf16),
            dma((chunks + 1,)),
            dma((N_MOVES,)),
            dma((N_MOVES,)),
            dma((9,)),
            dma((groups, chunks)),
            dma((groups, chunks)),
            dma((SENDERS,)),
            dma((SENDERS,)),
        ],
        compiler_params=pltpu.CompilerParams(
            collective_id=0, has_side_effects=True, vmem_limit_bytes=58 * 2**20
        ),
        cost_estimate=pl.CostEstimate(
            flops=2 * group_q * local_e * (depth + 128),
            bytes_accessed=local_e * depth * 2 + local_e * CATEGORIES * 4,
            transcendentals=3 * group_q * local_e,
        ),
        name="prefilter",
    )(queries, exemplars, labels.T)
    risk, density = pl.pallas_call(
        split_kernel,
        out_shape=(
            jax.ShapeDtypeStruct((local_q, CATEGORIES), f32),
            jax.ShapeDtypeStruct((1, local_q), f32),
        ),
        in_specs=[here],
        out_specs=(here, here),
        name="split",
    )(result)
    return risk, density.reshape(local_q)


def solution(mesh):
    in_specs = (P(("grp", "idx"), None), P("idx", None), P("idx", None))
    out_specs = (P(("grp", "idx"), None), P(("grp", "idx")))
    return jax.shard_map(
        per_device, mesh=mesh, in_specs=in_specs, out_specs=out_specs, check_vma=False
    )
```
